32 devices in a mesh: frame: 8 (over y, x, core), space: 4 (over z).
Axes of the slice: x: 2, y: 2, z: 4, core: 2. Of those that a mesh axis runs over, the one named last changes fastest.
Arguments:
- query_tokens: bfloat16 [8, 1024, 2240], P('frame', 'space'), may hold values from -6 to 6
- key_tokens: bfloat16 [8, 1024, 2240], P('frame', 'space'), may hold values from -500 to 500
- value_tokens: bfloat16 [8, 1024, 2240], P('frame', 'space'), may hold values from -6 to 6
- out_grad: bfloat16 [8, 1024, 2240], P('frame', 'space'), may hold values from -768 to 768
Outputs:
- query_grad: float32 [8, 1024, 2240], P('frame', 'space')
- key_grad: float32 [8, 1024, 2240], P('frame', 'space')
- value_grad: float32 [8, 1024, 2240], P('frame', 'space')
The draws below stay inside these ranges and needn't reach their ends.
All inputs are finite; a program needn't handle non-finite values.
Results may differ from the reference program's by a relative error of at most 0.0041.
Values sent between devices are 32-bit elements; how exact they have to be, the bound alone decides.
A program may use at most 128 MiB of HBM per device.

```python
import math
import jax
import jax.numpy as jnp
from jax import lax

HEADS = 20
HEAD_DIM = 112
WIDTH = 2240
SPACE_TOK = 1024
BLOCKS = 8


def draw_key_tokens(key, part):
    first, second, third = jax.random.split(key, 3)
    rows = jnp.exp(jax.random.uniform(second, (BLOCKS, SPACE_TOK, 1), minval=0.0, maxval=math.log(10.0)))
    columns = jnp.exp(jax.random.uniform(third, (WIDTH,), minval=0.0, maxval=math.log(10.0)))
    base = jnp.clip(jax.random.normal(first, (BLOCKS, SPACE_TOK, WIDTH)), -4.0, 4.0)
    result = base * rows * columns[None, None, :]
    return result.astype(jnp.bfloat16)


def level_of(stream_key, extent, shards, least, top_value):
    def one(dim, parts):
        steps = jax.random.uniform(jax.random.fold_in(jax.random.fold_in(stream_key, 6), dim), (parts,), jnp.float32, least / len(shards), top_value / len(shards))
        return jnp.repeat(jnp.exp(steps), extent[dim] // parts).reshape((-1,) + (1,) * (len(extent) - dim - 1))

    loudness = one(*shards[0])
    for cut in shards[1:]:
        loudness = loudness * one(*cut)
    return loudness


def scatter_about(key, extent, scale, reach, cuts=(), kind=jnp.bfloat16):
    level = level_of(key, extent, cuts, -0.22, 0.18) if cuts else 1.0
    values = jax.random.normal(key, extent, jnp.float32) * scale * level
    return jnp.minimum(jnp.maximum(values, -reach), reach).astype(kind)


def setup_inputs(seed: int = 0) -> dict:
    seeds = jax.random.split(jax.random.key(seed), 5)
    query_tokens = scatter_about(seeds[0], (BLOCKS, SPACE_TOK, WIDTH), 1.0, 6.0, ((0, 8), (1, 4)))
    key_tokens = draw_key_tokens(jax.random.fold_in(seeds[4], 71), 0)
    value_tokens = scatter_about(seeds[2], (BLOCKS, SPACE_TOK, WIDTH), 1.0, 6.0, ((0, 8), (1, 4)))
    out_grad = scatter_about(seeds[3], (BLOCKS, SPACE_TOK, WIDTH), 128.0, 768.0, ((0, 8), (1, 4)))
    return dict(query_tokens=query_tokens, key_tokens=key_tokens, value_tokens=value_tokens, out_grad=out_grad)


HIGH = lax.Precision.HIGHEST


def block_state(block):
    key_block, value_block = block
    k_feat = jnp.maximum(key_block, 0).astype(jnp.float32).reshape(SPACE_TOK, HEADS, HEAD_DIM)
    v_heads = value_block.astype(jnp.float32).reshape(SPACE_TOK, HEADS, HEAD_DIM)
    local_state = jnp.einsum("thi,thj->ihj", k_feat, v_heads, precision=HIGH)
    local_z = jnp.sum(k_feat, axis=0).T
    return local_state, local_z


def query_phase(block):
    query_block, grad_block, state, zsum = block
    q_heads = query_block.reshape(SPACE_TOK, HEADS, HEAD_DIM)
    q_feat = jnp.maximum(q_heads, 0).astype(jnp.float32)
    out_heads = grad_block.astype(jnp.float32).reshape(SPACE_TOK, HEADS, HEAD_DIM)
    numerator = jnp.einsum("thi,ihj->thj", q_feat, state, precision=HIGH)
    denominator = jnp.einsum("thi,ih->th", q_feat, zsum, precision=HIGH) + 1.0
    scaled = (out_heads / denominator[:, :, None]).astype(jnp.bfloat16)
    scaled = lax.optimization_barrier(scaled).astype(jnp.float32)
    denom_grad = -jnp.sum(out_heads * numerator, axis=-1) / (denominator * denominator)
    direct = jnp.einsum("thj,ihj->thi", scaled, state, precision=HIGH)
    query_grad = jnp.where(q_heads > 0, direct + denom_grad[:, :, None] * zsum.T[None], 0.0)
    local_grad = jnp.einsum("thi,thj->ihj", q_feat, scaled, precision=HIGH)
    local_zgrad = jnp.einsum("thi,th->ih", q_feat, denom_grad, precision=HIGH)
    return query_grad.reshape(SPACE_TOK, WIDTH), local_grad, local_zgrad


def key_phase(block):
    key_block, value_block, state_grad, zsum_grad = block
    k_heads = key_block.reshape(SPACE_TOK, HEADS, HEAD_DIM)
    k_feat = jnp.maximum(k_heads, 0).astype(jnp.float32)
    v_heads = value_block.astype(jnp.float32).reshape(SPACE_TOK, HEADS, HEAD_DIM)
    value_grad = jnp.einsum("thi,ihj->thj", k_feat, state_grad, precision=HIGH)
    key_part = jnp.einsum("thj,ihj->thi", v_heads, state_grad, precision=HIGH)
    key_grad = jnp.where(k_heads > 0, key_part + zsum_grad.T[None], 0.0)
    return key_grad.reshape(SPACE_TOK, WIDTH), value_grad.reshape(SPACE_TOK, WIDTH)


def reference(query_tokens, key_tokens, value_tokens, out_grad):
    local_state, local_z = lax.map(block_state, (key_tokens, value_tokens))
    state = jnp.cumsum(local_state, axis=0)
    zsum = jnp.cumsum(local_z, axis=0)
    query_grad, local_grad, local_zgrad = lax.map(query_phase, (query_tokens, out_grad, state, zsum))
    state_grad = jnp.flip(jnp.cumsum(jnp.flip(local_grad, 0), axis=0), 0)
    zsum_grad = jnp.flip(jnp.cumsum(jnp.flip(local_zgrad, 0), axis=0), 0)
    key_grad, value_grad = lax.map(key_phase, (key_tokens, value_tokens, state_grad, zsum_grad))
    return query_grad, key_grad, value_grad
```

```python
import functools

import jax
import jax.numpy as jnp
from jax import lax
from jax.experimental import pallas as pl
from jax.experimental.pallas import tpu as pltpu
from jax.sharding import PartitionSpec as P

HEADS = 20
HEAD_DIM = 112
LANES = 128
MESH = pl.DeviceIdType.MESH
NT = (((1,), (1,)), ((), ()))
TN = (((0,), (0,)), ((), ()))


def dot(a, b, dims=(((1,), (0,)), ((), ()))):
    return lax.dot_general(a, b, dims, preferred_element_type=jnp.float32)


def split(state):
    high = state.astype(jnp.bfloat16)
    low = (state - high.astype(jnp.float32)).astype(jnp.bfloat16)
    return jnp.concatenate([high, low], axis=1)


def twice(a):
    return jnp.concatenate([a, a], axis=1)


def kernel(
    n_frame, n_space,
    q_ref, k_ref, v_ref, g_ref,
    oq_ref, ok_ref, ov_ref,
    qs, ks, vs, gs, sq, sk, sv,
    local, prefix, total, arrived, send_sem, recv_sem,
):
    frame, space = lax.axis_index("frame"), lax.axis_index("space")
    levels = max(n_frame - 1, 0).bit_length()
    hops = levels + n_space - 1
    right_link, left_link = levels, levels + 1

    def place(phase):
        return frame if phase == 0 else n_frame - 1 - frame

    def partner(phase, level):
        at = place(phase)
        other = at ^ (1 << level)
        upper = lax.rem(at // (1 << level), 2) == 1
        exists = other < n_frame
        sends, receives = exists, exists
        if level == levels - 1:
            sends = jnp.logical_and(exists, jnp.logical_not(upper))
            receives = jnp.logical_and(exists, upper)
        return other if phase == 0 else n_frame - 1 - other, upper, exists, sends, receives

    def link(phase, number, h, source):
        if number == right_link:
            device = (frame, space + 1)
        elif number == left_link:
            device = (frame, space - 1)
        else:
            device = (partner(phase, number)[0], space)
        return pltpu.make_async_remote_copy(
            src_ref=source,
            dst_ref=arrived.at[phase, number, h],
            send_sem=send_sem.at[phase, number, h],
            recv_sem=recv_sem.at[phase, number, h],
            device_id=device,
            device_id_type=MESH,
        )

    barrier = pltpu.get_barrier_semaphore()
    greet = [(space + 1 < n_space, (frame, space + 1)), (space > 0, (frame, space - 1))]
    for phase in (0,) if n_frame & (n_frame - 1) == 0 else (0, 1):
        for level in range(levels):
            other, _, exists, _, _ = partner(phase, level)
            greet.append((exists, (other, space)))
    for exists, device in greet:
        @pl.when(exists)
        def _(device=device):
            pl.semaphore_signal(barrier, inc=1, device_id=device, device_id_type=MESH)

    rows = q_ref.shape[1]
    lane = lax.broadcasted_iota(jnp.int32, (rows, LANES), 1)
    extra = jnp.logical_or(lane == HEAD_DIM, lane == HEAD_DIM + 1)
    pad = jnp.zeros((rows, LANES - HEAD_DIM), jnp.bfloat16)
    ones = jnp.where(extra, 1.0, 0.0).astype(jnp.bfloat16)[:, HEAD_DIM:]
    for h in range(HEADS):
        cut = slice(h * HEAD_DIM, (h + 1) * HEAD_DIM)
        ks[h] = jnp.concatenate([jnp.maximum(k_ref[0, :, cut], 0), pad], axis=1)
        vs[h] = jnp.concatenate([v_ref[0, :, cut], ones], axis=1)
        qs[h] = jnp.concatenate([jnp.maximum(q_ref[0, :, cut], 0), pad], axis=1)
        gs[h] = jnp.concatenate([g_ref[0, :, cut], pad], axis=1)

    pl.semaphore_wait(barrier, sum(jnp.int32(exists) for exists, _ in greet))

    def begin(phase, h, value):
        local[phase, h] = value
        prefix[phase, h] = value
        if levels:
            sends = partner(phase, 0)[3]

            @pl.when(sends)
            def _():
                link(phase, 0, h, local.at[phase, h]).start()

    def scan_level(phase, level, h):
        _, upper, exists, sends, receives = partner(phase, level)
        source = local.at[phase, h] if level == 0 else arrived.at[phase, level - 1, h]

        @pl.when(receives)
        def _():
            link(phase, level, h, source).wait_recv()
            came = arrived[phase, level, h]

            @pl.when(upper)
            def _():
                prefix[phase, h] = prefix[phase, h] + came

            if level + 1 < levels:
                arrived[phase, level, h] = came + source[...]

        if level + 1 < levels:
            follows = partner(phase, level + 1)[3]

            @pl.when(follows)
            def _():
                link(phase, level + 1, h, arrived.at[phase, level, h]).start()

        if level + 1 == levels:
            begin_chain(phase, h)

    def begin_chain(phase, h):
        own = prefix.at[phase, h]
        total[phase, h] = own[...]
        if n_space > 1:
            @pl.when(space == 0)
            def _():
                link(phase, right_link, h, own).start()

            @pl.when(space == n_space - 1)
            def _():
                link(phase, left_link, h, own).start()

    def chain_hop(phase, hop, h):
        for number, at in ((right_link, space), (left_link, n_space - 1 - space)):
            @pl.when(at == hop)
            def _(number=number):
                slot = arrived.at[phase, number, h]
                link(phase, number, h, slot).wait_recv()
                came = slot[...]
                total[phase, h] = total[phase, h] + came
                if hop < n_space - 1:
                    slot[...] = came + prefix[phase, h]
                    link(phase, number, h, slot).start()

    def states(h):
        begin(0, h, dot(ks[h][:, :HEAD_DIM], vs[h], TN))

    def queries(h):
        q = qs[h][:, :HEAD_DIM]
        both = split(total[0, h])
        wide = dot(q, both)
        numerator = wide[:, :LANES] + wide[:, LANES:]
        denominator = numerator[:, HEAD_DIM:HEAD_DIM + 1] + 1.0
        grad = gs[h].astype(jnp.float32)
        slope = -jnp.sum(grad * numerator, axis=1, keepdims=True) / (denominator * denominator)
        coarse = slope.astype(jnp.bfloat16).astype(jnp.float32)
        scaled = jnp.where(lane == HEAD_DIM, coarse,
                           jnp.where(lane == HEAD_DIM + 1, slope - coarse, grad / denominator))
        scaled = scaled.astype(jnp.bfloat16)
        begin(1, h, dot(q, scaled, TN))
        back = dot(twice(scaled), both, NT)
        sq[h, :, :HEAD_DIM] = jnp.where(q.astype(jnp.float32) > 0, back, 0.0)

    def keys(h):
        k = ks[h][:, :HEAD_DIM]
        both = split(total[1, h])
        wide = dot(k, both)
        sv[h] = wide[:, :LANES] + wide[:, LANES:]
        back = dot(twice(vs[h]), both, NT)
        sk[h, :, :HEAD_DIM] = jnp.where(k.astype(jnp.float32) > 0, back, 0.0)

    def stage(t, lag, act):
        h = t - lag

        @pl.when(jnp.logical_and(h >= 0, h < HEADS))
        def _():
            act(h)

    def step(t, carry):
        for phase in (1, 0):
            for hop in range(n_space - 1, 0, -1):
                stage(t, phase * hops + levels + hop, functools.partial(chain_hop, phase, hop))
            for level in range(levels - 1, -1, -1):
                stage(t, phase * hops + level + 1, functools.partial(scan_level, phase, level))
        stage(t, 0, states)
        stage(t, hops, queries)
        stage(t, 2 * hops, keys)
        return carry

    lax.fori_loop(0, HEADS + 2 * hops, step, 0)

    for h in range(HEADS):
        cut = slice(h * HEAD_DIM, (h + 1) * HEAD_DIM)
        oq_ref[0, :, cut] = sq[h, :, :HEAD_DIM]
        ok_ref[0, :, cut] = sk[h, :, :HEAD_DIM]
        ov_ref[0, :, cut] = sv[h, :, :HEAD_DIM]

    def drain(h, carry):
        for phase in (0, 1):
            for level in range(levels):
                source = local.at[phase, h] if level == 0 else arrived.at[phase, level - 1, h]

                @pl.when(partner(phase, level)[3])
                def _(source=source, level=level):
                    link(phase, level, h, source).wait_send()
            for number, sends in ((right_link, space < n_space - 1), (left_link, space > 0)):
                @pl.when(sends)
                def _(number=number):
                    link(phase, number, h, prefix.at[phase, h]).wait_send()
        return carry

    lax.fori_loop(0, HEADS, drain, 0)


def on_device(n_frame, n_space, query_tokens, key_tokens, value_tokens, out_grad):
    shape = query_tokens.shape
    rows = shape[1]
    levels = max(n_frame - 1, 0).bit_length()
    out = jax.ShapeDtypeStruct(shape, jnp.float32)
    tokens = pltpu.VMEM((HEADS, rows, LANES), jnp.bfloat16)
    results = pltpu.VMEM((HEADS, rows, LANES), jnp.float32)
    state = (HEADS, HEAD_DIM, LANES)
    links = (2, levels + 2, HEADS)
    return pl.pallas_call(
        functools.partial(kernel, n_frame, n_space),
        out_shape=(out, out, out),
        in_specs=[pl.BlockSpec(memory_space=pltpu.VMEM)] * 4,
        out_specs=(pl.BlockSpec(memory_space=pltpu.VMEM),) * 3,
        scratch_shapes=[tokens] * 4 + [results] * 3 + [pltpu.VMEM((2,) + state, jnp.float32)] * 3 + [
            pltpu.VMEM((2, levels + 2) + state, jnp.float32),
            pltpu.SemaphoreType.DMA(links),
            pltpu.SemaphoreType.DMA(links),
        ],
        compiler_params=pltpu.CompilerParams(
            collective_id=0, has_side_effects=True, vmem_limit_bytes=60 * 1024 * 1024
        ),
    )(query_tokens, key_tokens, value_tokens, out_grad)


def solution(mesh):
    placed = P("frame", "space", None)
    return jax.shard_map(
        functools.partial(on_device, mesh.shape["frame"], mesh.shape["space"]),
        mesh=mesh,
        in_specs=(placed,) * 4,
        out_specs=(placed,) * 3,
        check_vma=False,
    )
```

```python
import functools

import jax
import jax.numpy as jnp
from jax import lax
from jax.experimental import pallas as pl
from jax.experimental.pallas import tpu as pltpu
from jax.sharding import PartitionSpec as P

HEADS = 20
HEAD_DIM = 112
LANES = 128
LAG = 2
MESH = pl.DeviceIdType.MESH
NT = (((1,), (1,)), ((), ()))
TN = (((0,), (0,)), ((), ()))


def dot(a, b, dims=(((1,), (0,)), ((), ()))):
    return lax.dot_general(a, b, dims, preferred_element_type=jnp.float32)


def split(state):
    high = state.astype(jnp.bfloat16)
    return high, (state - high.astype(jnp.float32)).astype(jnp.bfloat16)


def kernel(
    n_frame, n_space,
    q_in, k_in, v_in, g_in,
    oq_out, ok_out, ov_out,
    qs, ks, vs, gs, sq, sk, sv,
    local, prefix, total, arrived, send_sem, recv_sem, in_sem, out_sem,
):
    frame, space = lax.axis_index("frame"), lax.axis_index("space")
    levels = max(n_frame - 1, 0).bit_length()
    right_link, left_link = levels, levels + 1

    def place(phase):
        return frame if phase == 0 else n_frame - 1 - frame

    def partner(phase, level):
        at = place(phase)
        other = at ^ (1 << level)
        upper = lax.rem(at // (1 << level), 2) == 1
        exists = other < n_frame
        sends, receives = exists, exists
        if level == levels - 1:
            sends = jnp.logical_and(exists, jnp.logical_not(upper))
            receives = jnp.logical_and(exists, upper)
        return other if phase == 0 else n_frame - 1 - other, upper, exists, sends, receives

    def link(phase, number, h, source):
        if number == right_link:
            device = (frame, space + 1)
        elif number == left_link:
            device = (frame, space - 1)
        else:
            device = (partner(phase, number)[0], space)
        return pltpu.make_async_remote_copy(
            src_ref=source,
            dst_ref=arrived.at[phase, number, h],
            send_sem=send_sem.at[phase, number, h],
            recv_sem=recv_sem.at[phase, number, h],
            device_id=device,
            device_id_type=MESH,
        )

    barrier = pltpu.get_barrier_semaphore()
    greet = [(space + 1 < n_space, (frame, space + 1)), (space > 0, (frame, space - 1))]
    for phase in (0,) if n_frame & (n_frame - 1) == 0 else (0, 1):
        for level in range(levels):
            other, _, exists, _, _ = partner(phase, level)
            greet.append((exists, (other, space)))
    for exists, device in greet:
        @pl.when(exists)
        def _(device=device):
            pl.semaphore_signal(barrier, inc=1, device_id=device, device_id_type=MESH)

    loads = [
        pltpu.make_async_copy(source, target, in_sem.at[i])
        for i, (source, target) in enumerate(((k_in, ks), (v_in, vs), (q_in, qs), (g_in, gs)))
    ]
    for load in loads:
        load.start()

    def begin(phase, h, value):
        local[phase, h] = value
        if phase == 0:
            begin_chain(phase, h)
        else:
            begin_scan(phase, h)

    def begin_scan(phase, h):
        own = (total if phase == 0 else local).at[phase, h]
        prefix[phase, h] = own[...]
        if levels:
            @pl.when(partner(phase, 0)[3])
            def _():
                link(phase, 0, h, own).start()
        elif phase == 1:
            begin_chain(phase, h)

    def scan_source(phase, level, h):
        if level == 0:
            return (total if phase == 0 else local).at[phase, h]
        return arrived.at[phase, level - 1, h]

    def scan_level(phase, level, h):
        _, upper, exists, sends, receives = partner(phase, level)
        source = scan_source(phase, level, h)

        @pl.when(receives)
        def _():
            link(phase, level, h, source).wait_recv()
            came = arrived[phase, level, h]

            @pl.when(upper)
            def _():
                prefix[phase, h] = prefix[phase, h] + came

            if level + 1 < levels:
                arrived[phase, level, h] = came + source[...]

        if level + 1 < levels:
            @pl.when(partner(phase, level + 1)[3])
            def _():
                link(phase, level + 1, h, arrived.at[phase, level, h]).start()
        elif phase == 1:
            begin_chain(phase, h)

    def begin_chain(phase, h):
        own = (local if phase == 0 else prefix).at[phase, h]
        total[phase, h] = own[...]
        if n_space > 1:
            @pl.when(space == 0)
            def _():
                link(phase, right_link, h, own).start()

            @pl.when(space == n_space - 1)
            def _():
                link(phase, left_link, h, own).start()
        elif phase == 0:
            begin_scan(phase, h)

    def chain_hop(phase, hop, h):
        own = (local if phase == 0 else prefix).at[phase, h]
        for number, at in ((right_link, space), (left_link, n_space - 1 - space)):
            @pl.when(at == hop)
            def _(number=number):
                slot = arrived.at[phase, number, h]
                link(phase, number, h, slot).wait_recv()
                came = slot[...]
                total[phase, h] = total[phase, h] + came
                if hop < n_space - 1:
                    slot[...] = came + own[...]
                    link(phase, number, h, slot).start()
        if hop == n_space - 1 and phase == 0:
            begin_scan(phase, h)

    tokens = k_in.shape[2]
    rest = LANES - HEAD_DIM
    row = lax.broadcasted_iota(jnp.int32, (rest, tokens), 0)
    ones = jnp.where(row < 2, 1.0, 0.0).astype(jnp.bfloat16)

    def values(h):
        return jnp.concatenate([vs[h], ones], axis=0)

    def states(h):
        begin(0, h, dot(jnp.maximum(ks[h], 0), values(h), NT))

    def queries(h):
        q = jnp.maximum(qs[h], 0)
        high, low = split(prefix[0, h])
        numerator = dot(jnp.concatenate([high, low], axis=0), jnp.concatenate([q, q], axis=0), TN)
        denominator = numerator[HEAD_DIM:HEAD_DIM + 1] + 1.0
        grad = gs[h].astype(jnp.float32)
        slope = -jnp.sum(grad * numerator[:HEAD_DIM], axis=0, keepdims=True) / (denominator * denominator)
        coarse = slope.astype(jnp.bfloat16).astype(jnp.float32)
        slopes = jnp.where(row == 0, coarse, jnp.where(row == 1, slope - coarse, 0.0))
        scaled = jnp.concatenate([grad / denominator, slopes], axis=0).astype(jnp.bfloat16)
        begin(1, h, dot(q, scaled, NT))
        back = dot(jnp.concatenate([high, low], axis=1), jnp.concatenate([scaled, scaled], axis=0))
        sq[h] = jnp.where(q.astype(jnp.float32) > 0, back, 0.0)
        store(0, h).start()

    def keys(h):
        k = jnp.maximum(ks[h], 0)
        high, low = split(total[1, h])
        wide = dot(jnp.concatenate([high, low], axis=0), jnp.concatenate([k, k], axis=0), TN)
        sv[h] = wide[:HEAD_DIM]
        store(2, h).start()
        value = values(h)
        back = dot(jnp.concatenate([high, low], axis=1), jnp.concatenate([value, value], axis=0))
        sk[h] = jnp.where(k.astype(jnp.float32) > 0, back, 0.0)
        store(1, h).start()

    def store(i, h):
        source, target = ((sq, oq_out), (sk, ok_out), (sv, ov_out))[i]
        return pltpu.make_async_copy(source.at[h], target.at[h], out_sem.at[i, h])

    plan, at = [], 0
    for phase in (0, 1):
        scan = [(functools.partial(scan_level, phase, level), 1 if level == 0 else LAG) for level in range(levels)]
        chain = [(functools.partial(chain_hop, phase, hop), LAG) for hop in range(1, n_space)]
        for act, lag in chain + scan if phase == 0 else scan + chain:
            at += lag
            plan.append((at, act))
        if phase == 0:
            middle = at

    def stage(t, lag, act):
        h = t - lag

        @pl.when(jnp.logical_and(h >= 0, h < HEADS))
        def _():
            act(h)

    def step(t, carry):
        for lag, act in reversed(plan):
            stage(t, lag, act)
        stage(t, 0, states)

        @pl.when(t == middle)
        def _():
            loads[2].wait()
            loads[3].wait()

        stage(t, middle, queries)
        stage(t, at, keys)
        return carry

    loads[0].wait()
    loads[1].wait()
    pl.semaphore_wait(barrier, sum(jnp.int32(exists) for exists, _ in greet))
    lax.fori_loop(0, HEADS + at, step, 0)

    def drain(h, carry):
        for phase in (0, 1):
            for level in range(levels):
                source = scan_source(phase, level, h)

                @pl.when(partner(phase, level)[3])
                def _(source=source, level=level):
                    link(phase, level, h, source).wait_send()
            for number, sends in ((right_link, space < n_space - 1), (left_link, space > 0)):
                @pl.when(sends)
                def _(number=number):
                    link(phase, number, h, prefix.at[phase, h]).wait_send()
        for i in range(3):
            store(i, h).wait()
        return carry

    lax.fori_loop(0, HEADS, drain, 0)


def on_device(n_frame, n_space, *arrays):
    rows = arrays[0].shape[1]
    levels = max(n_frame - 1, 0).bit_length()
    heads = [jnp.swapaxes(array[0], 0, 1).reshape(HEADS, HEAD_DIM, rows) for array in arrays]
    shape = heads[0].shape
    out = jax.ShapeDtypeStruct(shape, jnp.float32)
    state = (HEADS, HEAD_DIM, LANES)
    links = (2, levels + 2, HEADS)
    grads = pl.pallas_call(
        functools.partial(kernel, n_frame, n_space),
        out_shape=(out,) * 3,
        in_specs=[pl.BlockSpec(memory_space=pl.ANY)] * 4,
        out_specs=(pl.BlockSpec(memory_space=pl.ANY),) * 3,
        scratch_shapes=[pltpu.VMEM(shape, jnp.bfloat16)] * 4 + [pltpu.VMEM(shape, jnp.float32)] * 3
        + [pltpu.VMEM((2,) + state, jnp.float32)] * 3
        + [
            pltpu.VMEM((2, levels + 2) + state, jnp.float32),
            pltpu.SemaphoreType.DMA(links),
            pltpu.SemaphoreType.DMA(links),
            pltpu.SemaphoreType.DMA((4,)),
            pltpu.SemaphoreType.DMA((3, HEADS)),
        ],
        compiler_params=pltpu.CompilerParams(
            collective_id=0, has_side_effects=True, vmem_limit_bytes=56 * 1024 * 1024
        ),
    )(*heads)
    return tuple(jnp.swapaxes(grad.reshape(HEADS * HEAD_DIM, rows), 0, 1)[None] for grad in grads)


def solution(mesh):
    placed = P("frame", "space", None)
    return jax.shard_map(
        functools.partial(on_device, mesh.shape["frame"], mesh.shape["space"]),
        mesh=mesh,
        in_specs=(placed,) * 4,
        out_specs=(placed,) * 3,
        check_vma=False,
    )
```

```python
import functools

import jax
import jax.numpy as jnp
from jax import lax
from jax.experimental import pallas as pl
from jax.experimental.pallas import tpu as pltpu
from jax.sharding import PartitionSpec as P

HEADS = 20
HEAD_DIM = 112
LANES = 128
LAG = 2
MESH = pl.DeviceIdType.MESH
NT = (((1,), (1,)), ((), ()))
TN = (((0,), (0,)), ((), ()))


def dot(a, b, dims=(((1,), (0,)), ((), ()))):
    return lax.dot_general(a, b, dims, preferred_element_type=jnp.float32)


def split(state):
    high = state.astype(jnp.bfloat16)
    return high, (state - high.astype(jnp.float32)).astype(jnp.bfloat16)


def guard(condition, act):
    if condition is True:
        act()
    else:
        pl.when(condition)(act)


def both(*conditions):
    left = [condition for condition in conditions if condition is not True]
    return functools.reduce(jnp.logical_and, left) if left else True


def ones_below(tokens):
    row = lax.broadcasted_iota(jnp.int32, (LANES - HEAD_DIM, tokens), 0)
    return row, jnp.where(row < 2, 1.0, 0.0).astype(jnp.bfloat16)


def kernel(
    n_frame, n_space,
    q_in, k_in, v_in, g_in,
    state_out, grad_out, scaled_out,
    qs, ks, vs, gs, scaleds,
    local, prefix, total, arrived, send_sem, recv_sem, in_sem, out_sem,
):
    frame, space = lax.axis_index("frame"), lax.axis_index("space")
    levels = max(n_frame - 1, 0).bit_length()
    right_link, left_link = levels, levels + 1

    def place(phase):
        return frame if phase == 0 else n_frame - 1 - frame

    def partner(phase, level):
        at = place(phase)
        other = at ^ (1 << level)
        upper = lax.rem(at // (1 << level), 2) == 1
        exists = True if n_frame & (n_frame - 1) == 0 else other < n_frame
        sends, receives = exists, exists
        if level == levels - 1:
            sends, receives = both(exists, jnp.logical_not(upper)), both(exists, upper)
        return other if phase == 0 else n_frame - 1 - other, upper, exists, sends, receives

    def link(phase, number, h, source):
        if number == right_link:
            device = (frame, space + 1)
        elif number == left_link:
            device = (frame, space - 1)
        else:
            device = (partner(phase, number)[0], space)
        return pltpu.make_async_remote_copy(
            src_ref=source,
            dst_ref=arrived.at[phase, number, h],
            send_sem=send_sem.at[phase, number, h],
            recv_sem=recv_sem.at[phase, number, h],
            device_id=device,
            device_id_type=MESH,
        )

    barrier = pltpu.get_barrier_semaphore()
    greet = [(space + 1 < n_space, (frame, space + 1)), (space > 0, (frame, space - 1))]
    for phase in (0,) if n_frame & (n_frame - 1) == 0 else (0, 1):
        for level in range(levels):
            other, _, exists, _, _ = partner(phase, level)
            greet.append((exists, (other, space)))
    for exists, device in greet:
        guard(exists, functools.partial(
            pl.semaphore_signal, barrier, inc=1, device_id=device, device_id_type=MESH))

    loads = [
        pltpu.make_async_copy(source, target, in_sem.at[i])
        for i, (source, target) in enumerate(((k_in, ks), (v_in, vs), (q_in, qs), (g_in, gs)))
    ]
    for load in loads:
        load.start()

    def begin(phase, h, value):
        local[phase, h] = value
        if phase == 0:
            begin_chain(phase, h)
        else:
            begin_scan(phase, h)

    def begin_scan(phase, h):
        own = scan_source(phase, 0, h)
        prefix[phase, h] = own[...]
        if levels:
            guard(partner(phase, 0)[3], lambda: link(phase, 0, h, own).start())
        elif phase == 1:
            begin_chain(phase, h)

    def scan_source(phase, level, h):
        if level == 0:
            return (total if phase == 0 else local).at[phase, h]
        return arrived.at[phase, level - 1, h]

    def scan_level(phase, level, h):
        _, upper, exists, sends, receives = partner(phase, level)
        source = scan_source(phase, level, h)

        def take():
            link(phase, level, h, source).wait_recv()
            came = arrived[phase, level, h]
            if level + 1 < levels:
                prefix[phase, h] = prefix[phase, h] + jnp.where(upper, came, 0.0)
                arrived[phase, level, h] = came + source[...]
            else:
                prefix[phase, h] = prefix[phase, h] + came

        guard(receives, take)
        if level + 1 < levels:
            follow = arrived.at[phase, level, h]
            guard(partner(phase, level + 1)[3], lambda: link(phase, level + 1, h, follow).start())
        elif phase == 1:
            begin_chain(phase, h)

    def chain_own(phase, h):
        return (local if phase == 0 else prefix).at[phase, h]

    def begin_chain(phase, h):
        own = chain_own(phase, h)
        total[phase, h] = own[...]
        if n_space > 1:
            guard(space == 0, lambda: link(phase, right_link, h, own).start())
            guard(space == n_space - 1, lambda: link(phase, left_link, h, own).start())

    def chain_hop(phase, number, at, h):
        slot = arrived.at[phase, number, h]
        link(phase, number, h, slot).wait_recv()
        came = slot[...]
        total[phase, h] = total[phase, h] + came

        def forward():
            slot[...] = came + chain_own(phase, h)[...]
            link(phase, number, h, slot).start()

        guard(at < n_space - 1, forward)

    tokens = k_in.shape[2]
    row, ones = ones_below(tokens)

    def values(h):
        return jnp.concatenate([vs[h], ones], axis=0)

    def states(h):
        begin(0, h, dot(jnp.maximum(ks[h], 0), values(h), NT))

    def queries(h):
        q = jnp.maximum(qs[h], 0)
        store(0, h).start()
        pair = jnp.concatenate(split(prefix[0, h]), axis=0)
        numerator = dot(pair, jnp.concatenate([q, q], axis=0), TN)
        inverse = 1.0 / (numerator[HEAD_DIM:HEAD_DIM + 1] + 1.0)
        grad = gs[h].astype(jnp.float32)
        slope = -jnp.sum(grad * numerator[:HEAD_DIM], axis=0, keepdims=True) * inverse * inverse
        coarse = slope.astype(jnp.bfloat16).astype(jnp.float32)
        slopes = jnp.where(row == 0, coarse, jnp.where(row == 1, slope - coarse, 0.0))
        scaled = jnp.concatenate([grad * inverse, slopes], axis=0).astype(jnp.bfloat16)
        begin(1, h, dot(q, scaled, NT))
        scaleds[h] = scaled
        store(2, h).start()

    def keys(h):
        store(1, h).start()

    def store(i, h):
        source, target = ((prefix.at[0], state_out), (total.at[1], grad_out), (scaleds, scaled_out))[i]
        return pltpu.make_async_copy(source.at[h], target.at[h], out_sem.at[i, h])

    plan = []

    def plan_scan(phase, at):
        for level in range(levels):
            at += 1 if level == 0 else LAG
            plan.insert(0, (at, True, functools.partial(scan_level, phase, level)))
        return at

    def plan_chain(phase, at):
        for number, place in ((right_link, space), (left_link, n_space - 1 - space)):
            if n_space > 1:
                plan.insert(0, (at + LAG * place, place > 0, functools.partial(chain_hop, phase, number, place)))
        return at + LAG * (n_space - 1)

    turn = plan_chain(0, 0)
    middle = plan_scan(0, turn)
    last = plan_chain(1, plan_scan(1, middle))

    def stage(t, lag, condition, act):
        h = t - lag
        guard(both(h >= 0, h < HEADS, condition), lambda: act(h))

    def step(t, carry):
        for lag, condition, act in plan:
            stage(t, lag, condition, act)
        stage(t, turn, True, functools.partial(begin_scan, 0))
        stage(t, 0, True, states)

        @pl.when(t == middle)
        def _():
            loads[2].wait()
            loads[3].wait()

        stage(t, middle, True, queries)
        stage(t, last, True, keys)
        return carry

    loads[0].wait()
    loads[1].wait()
    pl.semaphore_wait(barrier, sum(jnp.int32(exists) for exists, _ in greet))
    lax.fori_loop(0, HEADS + last, step, 0)

    def drain(h, carry):
        for phase in (0, 1):
            for level in range(levels):
                guard(partner(phase, level)[3], link(phase, level, h, scan_source(phase, level, h)).wait_send)
            own = chain_own(phase, h)
            if n_space > 1:
                guard(space < n_space - 1, link(phase, right_link, h, own).wait_send)
                guard(space > 0, link(phase, left_link, h, own).wait_send)
        for i in range(3):
            store(i, h).wait()
        return carry

    lax.fori_loop(0, HEADS, drain, 0)


def products(state, grad, scaled, q, k, v, query_grad, key_grad, value_grad):
    _, ones = ones_below(k.shape[2])
    for h in range(q.shape[0]):
        wide = jnp.concatenate(split(state[h]), axis=1)
        back = dot(wide, jnp.concatenate([scaled[h], scaled[h]], axis=0))
        query_grad[h] = jnp.where(q[h].astype(jnp.float32) > 0, back, 0.0)
        high, low = split(grad[h])
        feature = jnp.maximum(k[h], 0)
        value_grad[h] = dot(
            jnp.concatenate([high[:, :HEAD_DIM], low[:, :HEAD_DIM]], axis=0),
            jnp.concatenate([feature, feature], axis=0), TN)
        value = jnp.concatenate([v[h], ones], axis=0)
        back = dot(jnp.concatenate([high, low], axis=1), jnp.concatenate([value, value], axis=0))
        key_grad[h] = jnp.where(k[h].astype(jnp.float32) > 0, back, 0.0)


def on_device(n_frame, n_space, *arrays):
    rows = arrays[0].shape[1]
    levels = max(n_frame - 1, 0).bit_length()
    heads = [jnp.swapaxes(array[0], 0, 1).reshape(HEADS, HEAD_DIM, rows) for array in arrays]
    shape = heads[0].shape
    state = (HEADS, HEAD_DIM, LANES)
    wide = (HEADS, LANES, rows)
    links = (2, levels + 2, HEADS)
    states = pl.pallas_call(
        functools.partial(kernel, n_frame, n_space),
        out_shape=(
            jax.ShapeDtypeStruct(state, jnp.float32),
            jax.ShapeDtypeStruct(state, jnp.float32),
            jax.ShapeDtypeStruct(wide, jnp.bfloat16),
        ),
        in_specs=[pl.BlockSpec(memory_space=pl.ANY)] * 4,
        out_specs=(pl.BlockSpec(memory_space=pl.ANY),) * 3,
        scratch_shapes=[pltpu.VMEM(shape, jnp.bfloat16)] * 4 + [pltpu.VMEM(wide, jnp.bfloat16)]
        + [pltpu.VMEM((2,) + state, jnp.float32)] * 3
        + [
            pltpu.VMEM((2, levels + 2) + state, jnp.float32),
            pltpu.SemaphoreType.DMA(links),
            pltpu.SemaphoreType.DMA(links),
            pltpu.SemaphoreType.DMA((4,)),
            pltpu.SemaphoreType.DMA((3, HEADS)),
        ],
        compiler_params=pltpu.CompilerParams(
            collective_id=0, has_side_effects=True, vmem_limit_bytes=40 * 1024 * 1024
        ),
    )(*heads)
    group = max(n for n in range(1, 6) if HEADS % n == 0)

    def some(whole):
        return pl.BlockSpec((group,) + whole[1:], lambda i: (i, 0, 0))

    grads = pl.pallas_call(
        products,
        grid=(HEADS // group,),
        out_shape=(jax.ShapeDtypeStruct(shape, jnp.float32),) * 3,
        in_specs=[some(state), some(state), some(wide)] + [some(shape)] * 3,
        out_specs=(some(shape),) * 3,
        compiler_params=pltpu.CompilerParams(vmem_limit_bytes=24 * 1024 * 1024),
    )(*states, *heads[:3])
    return tuple(jnp.swapaxes(grad.reshape(HEADS * HEAD_DIM, rows), 0, 1)[None] for grad in grads)


def solution(mesh):
    placed = P("frame", "space", None)
    return jax.shard_map(
        functools.partial(on_device, mesh.shape["frame"], mesh.shape["space"]),
        mesh=mesh,
        in_specs=(placed,) * 4,
        out_specs=(placed,) * 3,
        check_vma=False,
    )
```

```python
import functools

import jax
import jax.numpy as jnp
from jax import lax
from jax.experimental import pallas as pl
from jax.experimental.pallas import tpu as pltpu
from jax.sharding import PartitionSpec as P

HEADS = 20
HEAD_DIM = 112
LANES = 128
LAG = 2
GROUP = 5
MESH = pl.DeviceIdType.MESH
NT = (((1,), (1,)), ((), ()))
TN = (((0,), (0,)), ((), ()))


def dot(a, b, dims=(((1,), (0,)), ((), ()))):
    return lax.dot_general(a, b, dims, preferred_element_type=jnp.float32)


def split(state):
    high = state.astype(jnp.bfloat16)
    return high, (state - high.astype(jnp.float32)).astype(jnp.bfloat16)


def guard(condition, act):
    if condition is True:
        act()
    else:
        pl.when(condition)(act)


def both(*conditions):
    left = [condition for condition in conditions if condition is not True]
    return functools.reduce(jnp.logical_and, left) if left else True


def ones_below(tokens):
    row = lax.broadcasted_iota(jnp.int32, (LANES - HEAD_DIM, tokens), 0)
    return row, jnp.where(row < 2, 1.0, 0.0).astype(jnp.bfloat16)


def kernel(
    n_frame, n_space,
    q_in, k_in, v_in, g_in,
    state_out, grad_out, scaled_out,
    qs, ks, vs, gs, scaleds,
    local, prefix, total, arrived, send_sem, recv_sem, in_sem, out_sem,
):
    frame, space = lax.axis_index("frame"), lax.axis_index("space")
    levels = max(n_frame - 1, 0).bit_length()
    right_link, left_link = levels, levels + 1

    def place(phase):
        return frame if phase == 0 else n_frame - 1 - frame

    def partner(phase, level):
        at = place(phase)
        other = at ^ (1 << level)
        upper = lax.rem(at // (1 << level), 2) == 1
        exists = True if n_frame & (n_frame - 1) == 0 else other < n_frame
        sends, receives = exists, exists
        if level == levels - 1:
            sends, receives = both(exists, jnp.logical_not(upper)), both(exists, upper)
        return other if phase == 0 else n_frame - 1 - other, upper, exists, sends, receives

    def link(phase, number, h, source):
        if number == right_link:
            device = (frame, space + 1)
        elif number == left_link:
            device = (frame, space - 1)
        else:
            device = (partner(phase, number)[0], space)
        return pltpu.make_async_remote_copy(
            src_ref=source,
            dst_ref=arrived.at[phase, number, h],
            send_sem=send_sem.at[phase, number, h],
            recv_sem=recv_sem.at[phase, number, h],
            device_id=device,
            device_id_type=MESH,
        )

    barrier = pltpu.get_barrier_semaphore()
    greet = [(space + 1 < n_space, (frame, space + 1)), (space > 0, (frame, space - 1))]
    for phase in (0,) if n_frame & (n_frame - 1) == 0 else (0, 1):
        for level in range(levels):
            other, _, exists, _, _ = partner(phase, level)
            greet.append((exists, (other, space)))
    for exists, device in greet:
        guard(exists, functools.partial(
            pl.semaphore_signal, barrier, inc=1, device_id=device, device_id_type=MESH))

    def load(i, part):
        source, target = ((k_in, ks), (v_in, vs), (q_in, qs), (g_in, gs))[i]
        some = pl.ds(part * GROUP, GROUP)
        return pltpu.make_async_copy(source.at[some], target.at[some], in_sem.at[i, part])

    for pair in ((0, 1), (2, 3)):
        for part in range(HEADS // GROUP):
            for i in pair:
                load(i, part).start()

    def loaded(pair, h):
        @pl.when(lax.rem(h, GROUP) == 0)
        def _():
            for i in pair:
                load(i, h // GROUP).wait()

    def begin(phase, h, value):
        local[phase, h] = value
        if phase == 0:
            begin_chain(phase, h)
        else:
            begin_scan(phase, h)

    def begin_scan(phase, h):
        own = scan_source(phase, 0, h)
        prefix[phase, h] = own[...]
        if levels:
            guard(partner(phase, 0)[3], lambda: link(phase, 0, h, own).start())
        elif phase == 1:
            begin_chain(phase, h)

    def scan_source(phase, level, h):
        if level == 0:
            return (total if phase == 0 else local).at[phase, h]
        return arrived.at[phase, level - 1, h]

    def scan_level(phase, level, h):
        _, upper, exists, sends, receives = partner(phase, level)
        source = scan_source(phase, level, h)

        def take():
            link(phase, level, h, source).wait_recv()
            came = arrived[phase, level, h]
            if level + 1 < levels:
                prefix[phase, h] = prefix[phase, h] + jnp.where(upper, came, 0.0)
                arrived[phase, level, h] = came + source[...]
            else:
                prefix[phase, h] = prefix[phase, h] + came

        guard(receives, take)
        if level + 1 < levels:
            follow = arrived.at[phase, level, h]
            guard(partner(phase, level + 1)[3], lambda: link(phase, level + 1, h, follow).start())
        elif phase == 1:
            begin_chain(phase, h)

    def chain_own(phase, h):
        return (local if phase == 0 else prefix).at[phase, h]

    def begin_chain(phase, h):
        own = chain_own(phase, h)
        total[phase, h] = own[...]
        if n_space > 1:
            guard(space == 0, lambda: link(phase, right_link, h, own).start())
            guard(space == n_space - 1, lambda: link(phase, left_link, h, own).start())

    def chain_hop(phase, number, at, h):
        slot = arrived.at[phase, number, h]
        link(phase, number, h, slot).wait_recv()
        came = slot[...]
        total[phase, h] = total[phase, h] + came

        def forward():
            slot[...] = came + chain_own(phase, h)[...]
            link(phase, number, h, slot).start()

        guard(at < n_space - 1, forward)

    tokens = k_in.shape[2]
    row, ones = ones_below(tokens)

    def values(h):
        return jnp.concatenate([vs[h], ones], axis=0)

    def states(h):
        loaded((0, 1), h)
        begin(0, h, dot(jnp.maximum(ks[h], 0), values(h), NT))

    def queries(h):
        loaded((2, 3), h)
        q = jnp.maximum(qs[h], 0)
        store(0, h).start()
        pair = jnp.concatenate(split(prefix[0, h]), axis=0)
        numerator = dot(pair, jnp.concatenate([q, q], axis=0), TN)
        inverse = 1.0 / (numerator[HEAD_DIM:HEAD_DIM + 1] + 1.0)
        grad = gs[h].astype(jnp.float32)
        slope = -jnp.sum(grad * numerator[:HEAD_DIM], axis=0, keepdims=True) * inverse * inverse
        coarse = slope.astype(jnp.bfloat16).astype(jnp.float32)
        slopes = jnp.where(row == 0, coarse, jnp.where(row == 1, slope - coarse, 0.0))
        scaled = jnp.concatenate([grad * inverse, slopes], axis=0).astype(jnp.bfloat16)
        begin(1, h, dot(q, scaled, NT))
        scaleds[h] = scaled
        store(2, h).start()

    def keys(h):
        store(1, h).start()

    def store(i, h):
        source, target = ((prefix.at[0], state_out), (total.at[1], grad_out), (scaleds, scaled_out))[i]
        return pltpu.make_async_copy(source.at[h], target.at[h], out_sem.at[i, h])

    plan = []

    def plan_scan(phase, at):
        for level in range(levels):
            at += LAG
            plan.insert(0, (at, True, functools.partial(scan_level, phase, level)))
        return at

    def plan_chain(phase, at):
        for number, place in ((right_link, space), (left_link, n_space - 1 - space)):
            if n_space > 1:
                plan.insert(0, (at + LAG * place, place > 0, functools.partial(chain_hop, phase, number, place)))
        return at + LAG * (n_space - 1)

    turn = plan_chain(0, 0)
    middle = plan_scan(0, turn)
    last = plan_chain(1, plan_scan(1, middle))

    def stage(t, lag, condition, act):
        h = t - lag
        guard(both(h >= 0, h < HEADS, condition), lambda: act(h))

    def step(t, carry):
        for lag, condition, act in plan:
            stage(t, lag, condition, act)
        stage(t, turn, True, functools.partial(begin_scan, 0))
        stage(t, 0, True, states)
        stage(t, middle, True, queries)
        stage(t, last, True, keys)
        return carry

    pl.semaphore_wait(barrier, sum(jnp.int32(exists) for exists, _ in greet))
    lax.fori_loop(0, HEADS + last, step, 0)

    def drain(h, carry):
        for phase in (0, 1):
            for level in range(levels):
                guard(partner(phase, level)[3], link(phase, level, h, scan_source(phase, level, h)).wait_send)
            own = chain_own(phase, h)
            if n_space > 1:
                guard(space < n_space - 1, link(phase, right_link, h, own).wait_send)
                guard(space > 0, link(phase, left_link, h, own).wait_send)
        for i in range(3):
            store(i, h).wait()
        return carry

    lax.fori_loop(0, HEADS, drain, 0)


def products(state, grad, scaled, q, k, v, query_grad, key_grad, value_grad):
    _, ones = ones_below(k.shape[2])
    for h in range(q.shape[0]):
        wide = jnp.concatenate(split(state[h]), axis=1)
        back = dot(wide, jnp.concatenate([scaled[h], scaled[h]], axis=0))
        query_grad[h] = jnp.where(q[h].astype(jnp.float32) > 0, back, 0.0)
        high, low = split(grad[h])
        feature = jnp.maximum(k[h], 0)
        value_grad[h] = dot(
            jnp.concatenate([high[:, :HEAD_DIM], low[:, :HEAD_DIM]], axis=0),
            jnp.concatenate([feature, feature], axis=0), TN)
        value = jnp.concatenate([v[h], ones], axis=0)
        back = dot(jnp.concatenate([high, low], axis=1), jnp.concatenate([value, value], axis=0))
        key_grad[h] = jnp.where(k[h].astype(jnp.float32) > 0, back, 0.0)


def on_device(n_frame, n_space, *arrays):
    rows = arrays[0].shape[1]
    levels = max(n_frame - 1, 0).bit_length()
    heads = [jnp.swapaxes(array[0], 0, 1).reshape(HEADS, HEAD_DIM, rows) for array in arrays]
    shape = heads[0].shape
    state = (HEADS, HEAD_DIM, LANES)
    wide = (HEADS, LANES, rows)
    links = (2, levels + 2, HEADS)
    states = pl.pallas_call(
        functools.partial(kernel, n_frame, n_space),
        out_shape=(
            jax.ShapeDtypeStruct(state, jnp.float32),
            jax.ShapeDtypeStruct(state, jnp.float32),
            jax.ShapeDtypeStruct(wide, jnp.bfloat16),
        ),
        in_specs=[pl.BlockSpec(memory_space=pltpu.HBM)] * 4,
        out_specs=(pl.BlockSpec(memory_space=pl.ANY),) * 3,
        scratch_shapes=[pltpu.VMEM(shape, jnp.bfloat16)] * 4 + [pltpu.VMEM(wide, jnp.bfloat16)]
        + [pltpu.VMEM((2,) + state, jnp.float32)] * 3
        + [
            pltpu.VMEM((2, levels + 2) + state, jnp.float32),
            pltpu.SemaphoreType.DMA(links),
            pltpu.SemaphoreType.DMA(links),
            pltpu.SemaphoreType.DMA((4, HEADS // GROUP)),
            pltpu.SemaphoreType.DMA((3, HEADS)),
        ],
        compiler_params=pltpu.CompilerParams(
            collective_id=0, has_side_effects=True, vmem_limit_bytes=56 * 1024 * 1024
        ),
    )(*heads)
    def some(whole):
        return pl.BlockSpec((GROUP,) + whole[1:], lambda i: (i, 0, 0))

    grads = pl.pallas_call(
        products,
        grid=(HEADS // GROUP,),
        out_shape=(jax.ShapeDtypeStruct(shape, jnp.float32),) * 3,
        in_specs=[some(state), some(state), some(wide)] + [some(shape)] * 3,
        out_specs=(some(shape),) * 3,
        compiler_params=pltpu.CompilerParams(vmem_limit_bytes=24 * 1024 * 1024),
    )(*states, *heads[:3])
    return tuple(jnp.swapaxes(grad.reshape(HEADS * HEAD_DIM, rows), 0, 1)[None] for grad in grads)


def solution(mesh):
    placed = P("frame", "space", None)
    return jax.shard_map(
        functools.partial(on_device, mesh.shape["frame"], mesh.shape["space"]),
        mesh=mesh,
        in_specs=(placed,) * 4,
        out_specs=(placed,) * 3,
        check_vma=False,
    )
```

```python
import functools

import jax
import jax.numpy as jnp
from jax import lax
from jax.experimental import pallas as pl
from jax.experimental.pallas import tpu as pltpu
from jax.sharding import PartitionSpec as P

HEADS = 20
HEAD_DIM = 112
LANES = 128
LAG = 2
GROUP = 5
MESH = pl.DeviceIdType.MESH
NT = (((1,), (1,)), ((), ()))
TN = (((0,), (0,)), ((), ()))


def dot(a, b, dims=(((1,), (0,)), ((), ()))):
    return lax.dot_general(a, b, dims, preferred_element_type=jnp.float32)


def split(state):
    high = state.astype(jnp.bfloat16)
    return high, (state - high.astype(jnp.float32)).astype(jnp.bfloat16)


def guard(condition, act):
    if condition is True:
        act()
    else:
        pl.when(condition)(act)


def both(*conditions):
    left = [condition for condition in conditions if condition is not True]
    return functools.reduce(jnp.logical_and, left) if left else True


def ones_below(tokens):
    row = lax.broadcasted_iota(jnp.int32, (LANES - HEAD_DIM, tokens), 0)
    return row, jnp.where(row < 2, 1.0, 0.0).astype(jnp.bfloat16)


def kernel(
    n_frame, n_space,
    q_in, k_in, v_in, g_in,
    state_out, grad_out, scaled_out,
    qs, ks, vs, gs, scaleds,
    local, prefix, total, arrived, send_sem, recv_sem, share_send, share_recv, in_sem, out_sem,
):
    frame, space = lax.axis_index("frame"), lax.axis_index("space")
    levels = max(n_frame - 1, 0).bit_length()
    right_link, left_link = levels, levels + 1

    def place(phase):
        return frame if phase == 0 else n_frame - 1 - frame

    def partner(phase, level):
        at = place(phase)
        other = at ^ (1 << level)
        upper = lax.rem(at // (1 << level), 2) == 1
        exists = True if n_frame & (n_frame - 1) == 0 else other < n_frame
        sends, receives = exists, exists
        if level == levels - 1:
            sends, receives = both(exists, jnp.logical_not(upper)), both(exists, upper)
        return other if phase == 0 else n_frame - 1 - other, upper, exists, sends, receives

    def halves(level):
        return 0 < level < levels and n_frame % 2 == 0

    def half(phase):
        rows = HEAD_DIM // 2
        return pl.ds(pl.multiple_of(lax.rem(place(phase), 2) * rows, 8), rows)

    def share(phase, level, h):
        part = arrived.at[phase, level, h, half(phase)]
        return pltpu.make_async_remote_copy(
            src_ref=part,
            dst_ref=part,
            send_sem=share_send.at[phase, level, h],
            recv_sem=share_recv.at[phase, level, h],
            device_id=(partner(phase, 0)[0], space),
            device_id_type=MESH,
        )

    def link(phase, number, h, source):
        if number == right_link:
            device = (frame, space + 1)
        elif number == left_link:
            device = (frame, space - 1)
        else:
            device = (partner(phase, number)[0], space)
        target = arrived.at[phase, number, h]
        if halves(number):
            source, target = source.at[half(phase)], target.at[half(phase)]
        return pltpu.make_async_remote_copy(
            src_ref=source,
            dst_ref=target,
            send_sem=send_sem.at[phase, number, h],
            recv_sem=recv_sem.at[phase, number, h],
            device_id=device,
            device_id_type=MESH,
        )

    barrier = pltpu.get_barrier_semaphore()
    greet = [(space + 1 < n_space, (frame, space + 1)), (space > 0, (frame, space - 1))]
    for phase in (0,) if n_frame & (n_frame - 1) == 0 else (0, 1):
        for level in range(levels):
            other, _, exists, _, _ = partner(phase, level)
            greet.append((exists, (other, space)))
    for exists, device in greet:
        guard(exists, functools.partial(
            pl.semaphore_signal, barrier, inc=1, device_id=device, device_id_type=MESH))

    def load(i, part):
        source, target = ((k_in, ks), (v_in, vs), (q_in, qs), (g_in, gs))[i]
        some = pl.ds(part * GROUP, GROUP)
        return pltpu.make_async_copy(source.at[some], target.at[some], in_sem.at[i, part])

    for pair in ((0, 1), (2, 3)):
        for part in range(HEADS // GROUP):
            for i in pair:
                load(i, part).start()

    def loaded(pair, h):
        @pl.when(lax.rem(h, GROUP) == 0)
        def _():
            for i in pair:
                load(i, h // GROUP).wait()

    def begin(phase, h, value):
        local[phase, h] = value
        if phase == 0:
            begin_chain(phase, h)
        else:
            begin_scan(phase, h)

    def begin_scan(phase, h):
        own = scan_source(phase, 0, h)
        prefix[phase, h] = own[...]
        if levels:
            guard(partner(phase, 0)[3], lambda: link(phase, 0, h, own).start())
        elif phase == 1:
            begin_chain(phase, h)

    def scan_source(phase, level, h):
        if level == 0:
            return (total if phase == 0 else local).at[phase, h]
        return arrived.at[phase, level - 1, h]

    def pass_on(phase, level, h):
        def act():
            link(phase, level, h, scan_source(phase, level, h)).wait_recv()
            share(phase, level, h).start()

        guard(partner(phase, level)[4], act)

    def scan_level(phase, level, h):
        _, upper, exists, sends, receives = partner(phase, level)
        source = scan_source(phase, level, h)

        def take():
            if halves(level):
                share(phase, level, h).wait()
            else:
                link(phase, level, h, source).wait_recv()
            came = arrived[phase, level, h]
            if level + 1 < levels:
                prefix[phase, h] = prefix[phase, h] + jnp.where(upper, came, 0.0)
                arrived[phase, level, h] = came + source[...]
            else:
                prefix[phase, h] = prefix[phase, h] + came

        guard(receives, take)
        if level + 1 < levels:
            follow = arrived.at[phase, level, h]
            guard(partner(phase, level + 1)[3], lambda: link(phase, level + 1, h, follow).start())
        elif phase == 1:
            begin_chain(phase, h)

    def chain_own(phase, h):
        return (local if phase == 0 else prefix).at[phase, h]

    def begin_chain(phase, h):
        own = chain_own(phase, h)
        total[phase, h] = own[...]
        if n_space > 1:
            guard(space == 0, lambda: link(phase, right_link, h, own).start())
            guard(space == n_space - 1, lambda: link(phase, left_link, h, own).start())

    def chain_hop(phase, number, at, h):
        slot = arrived.at[phase, number, h]
        link(phase, number, h, slot).wait_recv()
        came = slot[...]
        total[phase, h] = total[phase, h] + came

        def forward():
            slot[...] = came + chain_own(phase, h)[...]
            link(phase, number, h, slot).start()

        guard(at < n_space - 1, forward)

    tokens = k_in.shape[2]
    row, ones = ones_below(tokens)

    def values(h):
        return jnp.concatenate([vs[h], ones], axis=0)

    def states(h):
        loaded((0, 1), h)
        begin(0, h, dot(jnp.maximum(ks[h], 0), values(h), NT))

    def queries(h):
        loaded((2, 3), h)
        q = jnp.maximum(qs[h], 0)
        store(0, h).start()
        pair = jnp.concatenate(split(prefix[0, h]), axis=0)
        numerator = dot(pair, jnp.concatenate([q, q], axis=0), TN)
        inverse = 1.0 / (numerator[HEAD_DIM:HEAD_DIM + 1] + 1.0)
        grad = gs[h].astype(jnp.float32)
        slope = -jnp.sum(grad * numerator[:HEAD_DIM], axis=0, keepdims=True) * inverse * inverse
        coarse = slope.astype(jnp.bfloat16).astype(jnp.float32)
        slopes = jnp.where(row == 0, coarse, jnp.where(row == 1, slope - coarse, 0.0))
        scaled = jnp.concatenate([grad * inverse, slopes], axis=0).astype(jnp.bfloat16)
        begin(1, h, dot(q, scaled, NT))
        scaleds[h] = scaled
        store(2, h).start()

    def keys(h):
        store(1, h).start()

    def store(i, h):
        source, target = ((prefix.at[0], state_out), (total.at[1], grad_out), (scaleds, scaled_out))[i]
        return pltpu.make_async_copy(source.at[h], target.at[h], out_sem.at[i, h])

    plan = []

    def plan_scan(phase, at):
        for level in range(levels):
            at += LAG
            if halves(level):
                plan.insert(0, (at, True, functools.partial(pass_on, phase, level)))
                at += 1
            plan.insert(0, (at, True, functools.partial(scan_level, phase, level)))
        return at

    def plan_chain(phase, at):
        for number, place in ((right_link, space), (left_link, n_space - 1 - space)):
            if n_space > 1:
                plan.insert(0, (at + LAG * place, place > 0, functools.partial(chain_hop, phase, number, place)))
        return at + LAG * (n_space - 1)

    turn = plan_chain(0, 0)
    middle = plan_scan(0, turn)
    last = plan_chain(1, plan_scan(1, middle))

    def stage(t, lag, condition, act):
        h = t - lag
        guard(both(h >= 0, h < HEADS, condition), lambda: act(h))

    def step(t, carry):
        for lag, condition, act in plan:
            stage(t, lag, condition, act)
        stage(t, turn, True, functools.partial(begin_scan, 0))
        stage(t, 0, True, states)
        stage(t, middle, True, queries)
        stage(t, last, True, keys)
        return carry

    pl.semaphore_wait(barrier, sum(jnp.int32(exists) for exists, _ in greet))
    lax.fori_loop(0, HEADS + last, step, 0)

    def drain(h, carry):
        for phase in (0, 1):
            for level in range(levels):
                guard(partner(phase, level)[3], link(phase, level, h, scan_source(phase, level, h)).wait_send)
            own = chain_own(phase, h)
            if n_space > 1:
                guard(space < n_space - 1, link(phase, right_link, h, own).wait_send)
                guard(space > 0, link(phase, left_link, h, own).wait_send)
        for i in range(3):
            store(i, h).wait()
        return carry

    lax.fori_loop(0, HEADS, drain, 0)


def products(state, grad, scaled, q, k, v, query_grad, key_grad, value_grad):
    _, ones = ones_below(k.shape[2])
    for h in range(q.shape[0]):
        wide = jnp.concatenate(split(state[h]), axis=1)
        back = dot(wide, jnp.concatenate([scaled[h], scaled[h]], axis=0))
        query_grad[h] = jnp.where(q[h].astype(jnp.float32) > 0, back, 0.0)
        high, low = split(grad[h])
        feature = jnp.maximum(k[h], 0)
        value_grad[h] = dot(
            jnp.concatenate([high[:, :HEAD_DIM], low[:, :HEAD_DIM]], axis=0),
            jnp.concatenate([feature, feature], axis=0), TN)
        value = jnp.concatenate([v[h], ones], axis=0)
        back = dot(jnp.concatenate([high, low], axis=1), jnp.concatenate([value, value], axis=0))
        key_grad[h] = jnp.where(k[h].astype(jnp.float32) > 0, back, 0.0)


def on_device(n_frame, n_space, *arrays):
    rows = arrays[0].shape[1]
    levels = max(n_frame - 1, 0).bit_length()
    heads = [jnp.swapaxes(array[0], 0, 1).reshape(HEADS, HEAD_DIM, rows) for array in arrays]
    shape = heads[0].shape
    state = (HEADS, HEAD_DIM, LANES)
    wide = (HEADS, LANES, rows)
    links = (2, levels + 2, HEADS)
    states = pl.pallas_call(
        functools.partial(kernel, n_frame, n_space),
        out_shape=(
            jax.ShapeDtypeStruct(state, jnp.float32),
            jax.ShapeDtypeStruct(state, jnp.float32),
            jax.ShapeDtypeStruct(wide, jnp.bfloat16),
        ),
        in_specs=[pl.BlockSpec(memory_space=pltpu.HBM)] * 4,
        out_specs=(pl.BlockSpec(memory_space=pl.ANY),) * 3,
        scratch_shapes=[pltpu.VMEM(shape, jnp.bfloat16)] * 4 + [pltpu.VMEM(wide, jnp.bfloat16)]
        + [pltpu.VMEM((2,) + state, jnp.float32)] * 3
        + [
            pltpu.VMEM((2, levels + 2) + state, jnp.float32),
            pltpu.SemaphoreType.DMA(links),
            pltpu.SemaphoreType.DMA(links),
            pltpu.SemaphoreType.DMA(links),
            pltpu.SemaphoreType.DMA(links),
            pltpu.SemaphoreType.DMA((4, HEADS // GROUP)),
            pltpu.SemaphoreType.DMA((3, HEADS)),
        ],
        compiler_params=pltpu.CompilerParams(
            collective_id=0, has_side_effects=True, vmem_limit_bytes=56 * 1024 * 1024
        ),
    )(*heads)
    def some(whole):
        return pl.BlockSpec((GROUP,) + whole[1:], lambda i: (i, 0, 0))

    grads = pl.pallas_call(
        products,
        grid=(HEADS // GROUP,),
        out_shape=(jax.ShapeDtypeStruct(shape, jnp.float32),) * 3,
        in_specs=[some(state), some(state), some(wide)] + [some(shape)] * 3,
        out_specs=(some(shape),) * 3,
        compiler_params=pltpu.CompilerParams(vmem_limit_bytes=56 * 1024 * 1024),
    )(*states, *heads[:3])
    return tuple(jnp.swapaxes(grad.reshape(HEADS * HEAD_DIM, rows), 0, 1)[None] for grad in grads)


def solution(mesh):
    placed = P("frame", "space", None)
    return jax.shard_map(
        functools.partial(on_device, mesh.shape["frame"], mesh.shape["space"]),
        mesh=mesh,
        in_specs=(placed,) * 4,
        out_specs=(placed,) * 3,
        check_vma=False,
    )
```

```python
import functools

import jax
import jax.numpy as jnp
from jax import lax
from jax.experimental import pallas as pl
from jax.experimental.pallas import tpu as pltpu
from jax.sharding import PartitionSpec as P

HEADS = 20
HEAD_DIM = 112
LANES = 128
LAG = 2
GROUP = 5
TILE = 8
BLOCK = LANES - HEAD_DIM
BODY = HEAD_DIM - BLOCK
MESH = pl.DeviceIdType.MESH
NT = (((1,), (1,)), ((), ()))
TN = (((0,), (0,)), ((), ()))


def dot(a, b, dims=(((1,), (0,)), ((), ()))):
    return lax.dot_general(a, b, dims, preferred_element_type=jnp.float32)


def split(state):
    high = state.astype(jnp.bfloat16)
    return high, (state - high.astype(jnp.float32)).astype(jnp.bfloat16)


def guard(condition, act):
    if condition is True:
        act()
    else:
        pl.when(condition)(act)


def both(*conditions):
    left = [condition for condition in conditions if condition is not True]
    return functools.reduce(jnp.logical_and, left) if left else True


def lanes(rows):
    return lax.broadcasted_iota(jnp.int32, (rows, LANES), 1)


def pack(state, column):
    bottom, spare = state[BODY:], lanes(BLOCK) >= HEAD_DIM
    pieces = [
        jnp.where(spare, pltpu.roll(bottom, HEAD_DIM - at, 1), state[at:at + BLOCK])
        for at in range(0, BODY, BLOCK)
    ]
    lane = lanes(TILE)
    tail = jnp.where(lane >= HEAD_DIM, pltpu.roll(bottom[:TILE], LANES - HEAD_DIM, 1), bottom[TILE:])
    for g in range(HEAD_DIM // TILE):
        tail = jnp.where(lane == g, column[g * TILE:(g + 1) * TILE], tail)
    return jnp.concatenate(pieces + [tail], axis=0)


def unpack(packed, copies):
    tail, lane = packed[BODY:], lanes(BLOCK)
    bottom = jnp.concatenate([pltpu.roll(tail, HEAD_DIM, 1), tail], axis=0)
    pieces = []
    for at in range(0, BODY, BLOCK):
        piece = packed[at:at + BLOCK]
        here = jnp.logical_and(lane >= at, lane < at + BLOCK)
        bottom = jnp.where(here, pltpu.roll(piece, LANES - HEAD_DIM + at, 1), bottom)
        pieces.append(piece)
    pieces.append(bottom)
    whole = []
    for i, piece in enumerate(pieces):
        g = i * BLOCK // TILE
        column = jnp.concatenate([tail[:, g:g + 1], tail[:, g + 1:g + 2]], axis=0)
        z = jnp.where(lane < HEAD_DIM + copies, column, 0.0)
        whole.append(jnp.where(lane < HEAD_DIM, piece, z))
    return jnp.concatenate(whole, axis=0)


def ones_below(tokens):
    row = lax.broadcasted_iota(jnp.int32, (LANES - HEAD_DIM, tokens), 0)
    return row, jnp.where(row < 2, 1.0, 0.0).astype(jnp.bfloat16)


def kernel(
    n_frame, n_space,
    q_in, k_in, v_in, g_in,
    state_out, grad_out, scaled_out,
    qs, ks, vs, gs, scaleds, plain,
    local, prefix, total, arrived, send_sem, recv_sem, in_sem, out_sem,
):
    frame, space = lax.axis_index("frame"), lax.axis_index("space")
    levels = max(n_frame - 1, 0).bit_length()
    right_link, left_link = levels, levels + 1

    def place(phase):
        return frame if phase == 0 else n_frame - 1 - frame

    def partner(phase, level):
        at = place(phase)
        other = at ^ (1 << level)
        upper = lax.rem(at // (1 << level), 2) == 1
        exists = True if n_frame & (n_frame - 1) == 0 else other < n_frame
        sends, receives = exists, exists
        if level == levels - 1:
            sends, receives = both(exists, jnp.logical_not(upper)), both(exists, upper)
        return other if phase == 0 else n_frame - 1 - other, upper, exists, sends, receives

    def link(phase, number, h, source):
        if number == right_link:
            device = (frame, space + 1)
        elif number == left_link:
            device = (frame, space - 1)
        else:
            device = (partner(phase, number)[0], space)
        return pltpu.make_async_remote_copy(
            src_ref=source,
            dst_ref=arrived.at[phase, number, h],
            send_sem=send_sem.at[phase, number, h],
            recv_sem=recv_sem.at[phase, number, h],
            device_id=device,
            device_id_type=MESH,
        )

    barrier = pltpu.get_barrier_semaphore()
    greet = [(space + 1 < n_space, (frame, space + 1)), (space > 0, (frame, space - 1))]
    for phase in (0,) if n_frame & (n_frame - 1) == 0 else (0, 1):
        for level in range(levels):
            other, _, exists, _, _ = partner(phase, level)
            greet.append((exists, (other, space)))
    for exists, device in greet:
        guard(exists, functools.partial(
            pl.semaphore_signal, barrier, inc=1, device_id=device, device_id_type=MESH))

    def load(i, part):
        source, target = ((k_in, ks), (v_in, vs), (q_in, qs), (g_in, gs))[i]
        some = pl.ds(part * GROUP, GROUP)
        return pltpu.make_async_copy(source.at[some], target.at[some], in_sem.at[i, part])

    for pair in ((0, 1), (2, 3)):
        for part in range(HEADS // GROUP):
            for i in pair:
                load(i, part).start()

    def loaded(pair, h):
        @pl.when(lax.rem(h, GROUP) == 0)
        def _():
            for i in pair:
                load(i, h // GROUP).wait()

    def begin(phase, h, value):
        local[phase, h] = value
        if phase == 0:
            begin_chain(phase, h)
        else:
            begin_scan(phase, h)

    def begin_scan(phase, h):
        own = scan_source(phase, 0, h)
        prefix[phase, h] = own[...]
        if levels:
            guard(partner(phase, 0)[3], lambda: link(phase, 0, h, own).start())
        elif phase == 1:
            begin_chain(phase, h)

    def scan_source(phase, level, h):
        if level == 0:
            return (total if phase == 0 else local).at[phase, h]
        return arrived.at[phase, level - 1, h]

    def scan_level(phase, level, h):
        _, upper, exists, sends, receives = partner(phase, level)
        source = scan_source(phase, level, h)

        def take():
            link(phase, level, h, source).wait_recv()
            came = arrived[phase, level, h]
            if level + 1 < levels:
                prefix[phase, h] = prefix[phase, h] + jnp.where(upper, came, 0.0)
                arrived[phase, level, h] = came + source[...]
            else:
                prefix[phase, h] = prefix[phase, h] + came

        guard(receives, take)
        if level + 1 < levels:
            follow = arrived.at[phase, level, h]
            guard(partner(phase, level + 1)[3], lambda: link(phase, level + 1, h, follow).start())
        elif phase == 1:
            begin_chain(phase, h)

    def chain_own(phase, h):
        return (local if phase == 0 else prefix).at[phase, h]

    def begin_chain(phase, h):
        own = chain_own(phase, h)
        total[phase, h] = own[...]
        if n_space > 1:
            guard(space == 0, lambda: link(phase, right_link, h, own).start())
            guard(space == n_space - 1, lambda: link(phase, left_link, h, own).start())

    def chain_hop(phase, number, at, h):
        slot = arrived.at[phase, number, h]
        link(phase, number, h, slot).wait_recv()
        came = slot[...]
        total[phase, h] = total[phase, h] + came

        def forward():
            slot[...] = came + chain_own(phase, h)[...]
            link(phase, number, h, slot).start()

        guard(at < n_space - 1, forward)

    tokens = k_in.shape[2]
    row, ones = ones_below(tokens)

    def values(h):
        return jnp.concatenate([vs[h], ones], axis=0)

    def states(h):
        loaded((0, 1), h)
        state = dot(jnp.maximum(ks[h], 0), values(h), NT)
        begin(0, h, pack(state, state[:, HEAD_DIM:HEAD_DIM + 1]))

    def queries(h):
        loaded((2, 3), h)
        q = jnp.maximum(qs[h], 0)
        state = unpack(prefix[0, h], 2)
        plain[0, h] = state
        store(0, h).start()
        pair = jnp.concatenate(split(state), axis=0)
        numerator = dot(pair, jnp.concatenate([q, q], axis=0), TN)
        inverse = 1.0 / (numerator[HEAD_DIM:HEAD_DIM + 1] + 1.0)
        grad = gs[h].astype(jnp.float32)
        slope = -jnp.sum(grad * numerator[:HEAD_DIM], axis=0, keepdims=True) * inverse * inverse
        coarse = slope.astype(jnp.bfloat16).astype(jnp.float32)
        slopes = jnp.where(row == 0, coarse, jnp.where(row == 1, slope - coarse, 0.0))
        scaled = jnp.concatenate([grad * inverse, slopes], axis=0).astype(jnp.bfloat16)
        grads = dot(q, scaled, NT)
        begin(1, h, pack(grads, grads[:, HEAD_DIM:HEAD_DIM + 1] + grads[:, HEAD_DIM + 1:HEAD_DIM + 2]))
        scaleds[h] = scaled
        store(2, h).start()

    def keys(h):
        plain[1, h] = unpack(total[1, h], 1)
        store(1, h).start()

    def store(i, h):
        source, target = ((plain.at[0], state_out), (plain.at[1], grad_out), (scaleds, scaled_out))[i]
        return pltpu.make_async_copy(source.at[h], target.at[h], out_sem.at[i, h])

    plan = []

    def plan_scan(phase, at):
        for level in range(levels):
            at += LAG
            plan.insert(0, (at, True, functools.partial(scan_level, phase, level)))
        return at

    def plan_chain(phase, at):
        for number, place in ((right_link, space), (left_link, n_space - 1 - space)):
            if n_space > 1:
                plan.insert(0, (at + LAG * place, place > 0, functools.partial(chain_hop, phase, number, place)))
        return at + LAG * (n_space - 1)

    turn = plan_chain(0, 0)
    middle = plan_scan(0, turn)
    last = plan_chain(1, plan_scan(1, middle))

    def stage(t, lag, condition, act):
        h = t - lag
        guard(both(h >= 0, h < HEADS, condition), lambda: act(h))

    def step(t, carry):
        for lag, condition, act in plan:
            stage(t, lag, condition, act)
        stage(t, turn, True, functools.partial(begin_scan, 0))
        stage(t, 0, True, states)
        stage(t, middle, True, queries)
        stage(t, last, True, keys)
        return carry

    pl.semaphore_wait(barrier, sum(jnp.int32(exists) for exists, _ in greet))
    lax.fori_loop(0, HEADS + last, step, 0)

    def drain(h, carry):
        for phase in (0, 1):
            for level in range(levels):
                guard(partner(phase, level)[3], link(phase, level, h, scan_source(phase, level, h)).wait_send)
            own = chain_own(phase, h)
            if n_space > 1:
                guard(space < n_space - 1, link(phase, right_link, h, own).wait_send)
                guard(space > 0, link(phase, left_link, h, own).wait_send)
        for i in range(3):
            store(i, h).wait()
        return carry

    lax.fori_loop(0, HEADS, drain, 0)


def products(state, grad, scaled, q, k, v, query_grad, key_grad, value_grad):
    _, ones = ones_below(k.shape[2])
    for h in range(q.shape[0]):
        wide = jnp.concatenate(split(state[h]), axis=1)
        back = dot(wide, jnp.concatenate([scaled[h], scaled[h]], axis=0))
        query_grad[h] = jnp.where(q[h].astype(jnp.float32) > 0, back, 0.0)
        high, low = split(grad[h])
        feature = jnp.maximum(k[h], 0)
        value_grad[h] = dot(
            jnp.concatenate([high[:, :HEAD_DIM], low[:, :HEAD_DIM]], axis=0),
            jnp.concatenate([feature, feature], axis=0), TN)
        value = jnp.concatenate([v[h], ones], axis=0)
        back = dot(jnp.concatenate([high, low], axis=1), jnp.concatenate([value, value], axis=0))
        key_grad[h] = jnp.where(k[h].astype(jnp.float32) > 0, back, 0.0)


def on_device(n_frame, n_space, *arrays):
    rows = arrays[0].shape[1]
    levels = max(n_frame - 1, 0).bit_length()
    heads = [jnp.swapaxes(array[0], 0, 1).reshape(HEADS, HEAD_DIM, rows) for array in arrays]
    shape = heads[0].shape
    state = (HEADS, HEAD_DIM, LANES)
    packed = (HEADS, BODY + TILE, LANES)
    wide = (HEADS, LANES, rows)
    links = (2, levels + 2, HEADS)
    states = pl.pallas_call(
        functools.partial(kernel, n_frame, n_space),
        out_shape=(
            jax.ShapeDtypeStruct(state, jnp.float32),
            jax.ShapeDtypeStruct(state, jnp.float32),
            jax.ShapeDtypeStruct(wide, jnp.bfloat16),
        ),
        in_specs=[pl.BlockSpec(memory_space=pltpu.HBM)] * 4,
        out_specs=(pl.BlockSpec(memory_space=pl.ANY),) * 3,
        scratch_shapes=[pltpu.VMEM(shape, jnp.bfloat16)] * 4 + [pltpu.VMEM(wide, jnp.bfloat16)]
        + [pltpu.VMEM((2,) + state, jnp.float32)] + [pltpu.VMEM((2,) + packed, jnp.float32)] * 3
        + [
            pltpu.VMEM((2, levels + 2) + packed, jnp.float32),
            pltpu.SemaphoreType.DMA(links),
            pltpu.SemaphoreType.DMA(links),
            pltpu.SemaphoreType.DMA((4, HEADS // GROUP)),
            pltpu.SemaphoreType.DMA((3, HEADS)),
        ],
        compiler_params=pltpu.CompilerParams(
            collective_id=0, has_side_effects=True, vmem_limit_bytes=56 * 1024 * 1024
        ),
    )(*heads)
    def some(whole):
        return pl.BlockSpec((GROUP,) + whole[1:], lambda i: (i, 0, 0))

    grads = pl.pallas_call(
        products,
        grid=(HEADS // GROUP,),
        out_shape=(jax.ShapeDtypeStruct(shape, jnp.float32),) * 3,
        in_specs=[some(state), some(state), some(wide)] + [some(shape)] * 3,
        out_specs=(some(shape),) * 3,
        compiler_params=pltpu.CompilerParams(vmem_limit_bytes=56 * 1024 * 1024),
    )(*states, *heads[:3])
    return tuple(jnp.swapaxes(grad.reshape(HEADS * HEAD_DIM, rows), 0, 1)[None] for grad in grads)


def solution(mesh):
    placed = P("frame", "space", None)
    return jax.shard_map(
        functools.partial(on_device, mesh.shape["frame"], mesh.shape["space"]),
        mesh=mesh,
        in_specs=(placed,) * 4,
        out_specs=(placed,) * 3,
        check_vma=False,
    )
```

```python
import functools

import jax
import jax.numpy as jnp
from jax import lax
from jax.experimental import pallas as pl
from jax.experimental.pallas import tpu as pltpu
from jax.sharding import PartitionSpec as P

HEADS = 20
HEAD_DIM = 112
LANES = 128
LAG = 3
GROUP = 5
TILE = 8
BLOCK = LANES - HEAD_DIM
BODY = HEAD_DIM - BLOCK
MESH = pl.DeviceIdType.MESH
NT = (((1,), (1,)), ((), ()))
TN = (((0,), (0,)), ((), ()))


def dot(a, b, dims=(((1,), (0,)), ((), ()))):
    return lax.dot_general(a, b, dims, preferred_element_type=jnp.float32)


def split(state):
    high = state.astype(jnp.bfloat16)
    return high, (state - high.astype(jnp.float32)).astype(jnp.bfloat16)


def guard(condition, act):
    if condition is True:
        act()
    else:
        pl.when(condition)(act)


def both(*conditions):
    left = [condition for condition in conditions if condition is not True]
    return functools.reduce(jnp.logical_and, left) if left else True


def lanes(rows):
    return lax.broadcasted_iota(jnp.int32, (rows, LANES), 1)


def pack(state, column):
    bottom, spare = state[BODY:], lanes(BLOCK) >= HEAD_DIM
    pieces = [
        jnp.where(spare, pltpu.roll(bottom, HEAD_DIM - at, 1), state[at:at + BLOCK])
        for at in range(0, BODY, BLOCK)
    ]
    lane = lanes(TILE)
    tail = jnp.where(lane >= HEAD_DIM, pltpu.roll(bottom[:TILE], LANES - HEAD_DIM, 1), bottom[TILE:])
    for g in range(HEAD_DIM // TILE):
        tail = jnp.where(lane == g, column[g * TILE:(g + 1) * TILE], tail)
    return jnp.concatenate(pieces + [tail], axis=0)


def unpack(packed, copies):
    tail, lane = packed[BODY:], lanes(BLOCK)
    bottom = jnp.concatenate([pltpu.roll(tail, HEAD_DIM, 1), tail], axis=0)
    pieces = []
    for at in range(0, BODY, BLOCK):
        piece = packed[at:at + BLOCK]
        here = jnp.logical_and(lane >= at, lane < at + BLOCK)
        bottom = jnp.where(here, pltpu.roll(piece, LANES - HEAD_DIM + at, 1), bottom)
        pieces.append(piece)
    pieces.append(bottom)
    whole = []
    for i, piece in enumerate(pieces):
        g = i * BLOCK // TILE
        column = jnp.concatenate([tail[:, g:g + 1], tail[:, g + 1:g + 2]], axis=0)
        z = jnp.where(lane < HEAD_DIM + copies, column, 0.0)
        whole.append(jnp.where(lane < HEAD_DIM, piece, z))
    return jnp.concatenate(whole, axis=0)


def ones_below(tokens):
    row = lax.broadcasted_iota(jnp.int32, (LANES - HEAD_DIM, tokens), 0)
    return row, jnp.where(row < 2, 1.0, 0.0).astype(jnp.bfloat16)


def kernel(
    n_frame, n_space,
    q_in, k_in, v_in, g_in,
    state_out, grad_out, scaled_out,
    qs, ks, vs, gs, scaleds, plain,
    local, prefix, total, arrived, send_sem, recv_sem, in_sem, out_sem,
):
    frame, space = lax.axis_index("frame"), lax.axis_index("space")
    levels = max(n_frame - 1, 0).bit_length()
    right_link, left_link = levels, levels + 1

    def place(phase):
        return frame if phase == 0 else n_frame - 1 - frame

    def partner(phase, level):
        at = place(phase)
        other = at ^ (1 << level)
        upper = lax.rem(at // (1 << level), 2) == 1
        exists = True if n_frame & (n_frame - 1) == 0 else other < n_frame
        sends, receives = exists, exists
        if level == levels - 1:
            sends, receives = both(exists, jnp.logical_not(upper)), both(exists, upper)
        return other if phase == 0 else n_frame - 1 - other, upper, exists, sends, receives

    def link(phase, number, h, source):
        if number == right_link:
            device = (frame, space + 1)
        elif number == left_link:
            device = (frame, space - 1)
        else:
            device = (partner(phase, number)[0], space)
        return pltpu.make_async_remote_copy(
            src_ref=source,
            dst_ref=arrived.at[phase, number, h],
            send_sem=send_sem.at[phase, number, h],
            recv_sem=recv_sem.at[phase, number, h],
            device_id=device,
            device_id_type=MESH,
        )

    barrier = pltpu.get_barrier_semaphore()
    greet = [(space + 1 < n_space, (frame, space + 1)), (space > 0, (frame, space - 1))]
    for phase in (0,) if n_frame & (n_frame - 1) == 0 else (0, 1):
        for level in range(levels):
            other, _, exists, _, _ = partner(phase, level)
            greet.append((exists, (other, space)))
    for exists, device in greet:
        guard(exists, functools.partial(
            pl.semaphore_signal, barrier, inc=1, device_id=device, device_id_type=MESH))

    def load(i, part):
        source, target = ((k_in, ks), (v_in, vs), (q_in, qs), (g_in, gs))[i]
        some = pl.ds(part * GROUP, GROUP)
        return pltpu.make_async_copy(source.at[some], target.at[some], in_sem.at[i, part])

    for pair in ((0, 1), (2, 3)):
        for part in range(HEADS // GROUP):
            for i in pair:
                load(i, part).start()

    def loaded(pair, h):
        @pl.when(lax.rem(h, GROUP) == 0)
        def _():
            for i in pair:
                load(i, h // GROUP).wait()

    def begin(phase, h, value):
        local[phase, h] = value
        if phase == 0:
            begin_chain(phase, h)
        else:
            begin_scan(phase, h)

    def begin_scan(phase, h):
        own = scan_source(phase, 0, h)
        prefix[phase, h] = own[...]
        if levels:
            guard(partner(phase, 0)[3], lambda: link(phase, 0, h, own).start())
        elif phase == 1:
            begin_chain(phase, h)

    def scan_source(phase, level, h):
        if level == 0:
            return (total if phase == 0 else local).at[phase, h]
        return arrived.at[phase, level - 1, h]

    def scan_level(phase, level, h):
        _, upper, exists, sends, receives = partner(phase, level)
        source = scan_source(phase, level, h)

        def take():
            link(phase, level, h, source).wait_recv()
            came = arrived[phase, level, h]
            if level + 1 < levels:
                prefix[phase, h] = prefix[phase, h] + jnp.where(upper, came, 0.0)
                arrived[phase, level, h] = came + source[...]
            else:
                prefix[phase, h] = prefix[phase, h] + came

        guard(receives, take)
        if level + 1 < levels:
            follow = arrived.at[phase, level, h]
            guard(partner(phase, level + 1)[3], lambda: link(phase, level + 1, h, follow).start())
        elif phase == 1:
            begin_chain(phase, h)

    def chain_own(phase, h):
        return (local if phase == 0 else prefix).at[phase, h]

    def begin_chain(phase, h):
        own = chain_own(phase, h)
        total[phase, h] = own[...]
        if n_space > 1:
            guard(space == 0, lambda: link(phase, right_link, h, own).start())
            guard(space == n_space - 1, lambda: link(phase, left_link, h, own).start())

    def chain_hop(phase, number, at, h):
        slot = arrived.at[phase, number, h]
        link(phase, number, h, slot).wait_recv()
        came = slot[...]
        total[phase, h] = total[phase, h] + came

        def forward():
            slot[...] = came + chain_own(phase, h)[...]
            link(phase, number, h, slot).start()

        guard(at < n_space - 1, forward)

    tokens = k_in.shape[2]
    row, ones = ones_below(tokens)

    def values(h):
        return jnp.concatenate([vs[h], ones], axis=0)

    def states(h):
        loaded((0, 1), h)
        state = dot(jnp.maximum(ks[h], 0), values(h), NT)
        begin(0, h, pack(state, state[:, HEAD_DIM:HEAD_DIM + 1]))

    def queries(h):
        loaded((2, 3), h)
        q = jnp.maximum(qs[h], 0)
        state = unpack(prefix[0, h], 2)
        plain[0, h] = state
        store(0, h).start()
        pair = jnp.concatenate(split(state), axis=0)
        numerator = dot(pair, jnp.concatenate([q, q], axis=0), TN)
        inverse = 1.0 / (numerator[HEAD_DIM:HEAD_DIM + 1] + 1.0)
        grad = gs[h].astype(jnp.float32)
        slope = -jnp.sum(grad * numerator[:HEAD_DIM], axis=0, keepdims=True) * inverse * inverse
        coarse = slope.astype(jnp.bfloat16).astype(jnp.float32)
        slopes = jnp.where(row == 0, coarse, jnp.where(row == 1, slope - coarse, 0.0))
        scaled = jnp.concatenate([grad * inverse, slopes], axis=0).astype(jnp.bfloat16)
        grads = dot(q, scaled, NT)
        begin(1, h, pack(grads, grads[:, HEAD_DIM:HEAD_DIM + 1] + grads[:, HEAD_DIM + 1:HEAD_DIM + 2]))
        scaleds[h] = scaled
        store(2, h).start()

    def keys(h):
        plain[1, h] = unpack(total[1, h], 1)
        store(1, h).start()

    def store(i, h):
        source, target = ((plain.at[0], state_out), (plain.at[1], grad_out), (scaleds, scaled_out))[i]
        return pltpu.make_async_copy(source.at[h], target.at[h], out_sem.at[i, h])

    plan = []

    def plan_scan(phase, at):
        for level in range(levels):
            at += LAG
            plan.insert(0, (at, True, functools.partial(scan_level, phase, level)))
        return at

    def plan_chain(phase, at):
        for number, place in ((right_link, space), (left_link, n_space - 1 - space)):
            if n_space > 1:
                plan.insert(0, (at + LAG * place, place > 0, functools.partial(chain_hop, phase, number, place)))
        return at + LAG * (n_space - 1)

    turn = plan_chain(0, 0)
    middle = plan_scan(0, turn)
    last = plan_chain(1, plan_scan(1, middle))

    def stage(t, lag, condition, act):
        h = t - lag
        guard(both(h >= 0, h < HEADS, condition), lambda: act(h))

    def step(t, carry):
        for lag, condition, act in plan:
            stage(t, lag, condition, act)
        stage(t, turn, True, functools.partial(begin_scan, 0))
        stage(t, 0, True, states)
        stage(t, middle, True, queries)
        stage(t, last, True, keys)
        return carry

    pl.semaphore_wait(barrier, sum(jnp.int32(exists) for exists, _ in greet))
    lax.fori_loop(0, HEADS + last, step, 0)

    def drain(h, carry):
        for phase in (0, 1):
            for level in range(levels):
                guard(partner(phase, level)[3], link(phase, level, h, scan_source(phase, level, h)).wait_send)
            own = chain_own(phase, h)
            if n_space > 1:
                guard(space < n_space - 1, link(phase, right_link, h, own).wait_send)
                guard(space > 0, link(phase, left_link, h, own).wait_send)
        for i in range(3):
            store(i, h).wait()
        return carry

    lax.fori_loop(0, HEADS, drain, 0)


def products(state, grad, scaled, q, k, v, query_grad, key_grad, value_grad):
    _, ones = ones_below(k.shape[2])
    for h in range(q.shape[0]):
        wide = jnp.concatenate(split(state[h]), axis=1)
        back = dot(wide, jnp.concatenate([scaled[h], scaled[h]], axis=0))
        query_grad[h] = jnp.where(q[h].astype(jnp.float32) > 0, back, 0.0)
        high, low = split(grad[h])
        feature = jnp.maximum(k[h], 0)
        value_grad[h] = dot(
            jnp.concatenate([high[:, :HEAD_DIM], low[:, :HEAD_DIM]], axis=0),
            jnp.concatenate([feature, feature], axis=0), TN)
        value = jnp.concatenate([v[h], ones], axis=0)
        back = dot(jnp.concatenate([high, low], axis=1), jnp.concatenate([value, value], axis=0))
        key_grad[h] = jnp.where(k[h].astype(jnp.float32) > 0, back, 0.0)


def on_device(n_frame, n_space, *arrays):
    rows = arrays[0].shape[1]
    levels = max(n_frame - 1, 0).bit_length()
    heads = [jnp.swapaxes(array[0], 0, 1).reshape(HEADS, HEAD_DIM, rows) for array in arrays]
    shape = heads[0].shape
    state = (HEADS, HEAD_DIM, LANES)
    packed = (HEADS, BODY + TILE, LANES)
    wide = (HEADS, LANES, rows)
    links = (2, levels + 2, HEADS)
    states = pl.pallas_call(
        functools.partial(kernel, n_frame, n_space),
        out_shape=(
            jax.ShapeDtypeStruct(state, jnp.float32),
            jax.ShapeDtypeStruct(state, jnp.float32),
            jax.ShapeDtypeStruct(wide, jnp.bfloat16),
        ),
        in_specs=[pl.BlockSpec(memory_space=pltpu.HBM)] * 4,
        out_specs=(pl.BlockSpec(memory_space=pl.ANY),) * 3,
        scratch_shapes=[pltpu.VMEM(shape, jnp.bfloat16)] * 4 + [pltpu.VMEM(wide, jnp.bfloat16)]
        + [pltpu.VMEM((2,) + state, jnp.float32)] + [pltpu.VMEM((2,) + packed, jnp.float32)] * 3
        + [
            pltpu.VMEM((2, levels + 2) + packed, jnp.float32),
            pltpu.SemaphoreType.DMA(links),
            pltpu.SemaphoreType.DMA(links),
            pltpu.SemaphoreType.DMA((4, HEADS // GROUP)),
            pltpu.SemaphoreType.DMA((3, HEADS)),
        ],
        compiler_params=pltpu.CompilerParams(
            collective_id=0, has_side_effects=True, vmem_limit_bytes=56 * 1024 * 1024
        ),
    )(*heads)
    def some(whole):
        return pl.BlockSpec((GROUP,) + whole[1:], lambda i: (i, 0, 0))

    grads = pl.pallas_call(
        products,
        grid=(HEADS // GROUP,),
        out_shape=(jax.ShapeDtypeStruct(shape, jnp.float32),) * 3,
        in_specs=[some(state), some(state), some(wide)] + [some(shape)] * 3,
        out_specs=(some(shape),) * 3,
        compiler_params=pltpu.CompilerParams(vmem_limit_bytes=56 * 1024 * 1024),
    )(*states, *heads[:3])
    return tuple(jnp.swapaxes(grad.reshape(HEADS * HEAD_DIM, rows), 0, 1)[None] for grad in grads)


def solution(mesh):
    placed = P("frame", "space", None)
    return jax.shard_map(
        functools.partial(on_device, mesh.shape["frame"], mesh.shape["space"]),
        mesh=mesh,
        in_specs=(placed,) * 4,
        out_specs=(placed,) * 3,
        check_vma=False,
    )
```

```python
import functools

import jax
import jax.numpy as jnp
from jax import lax
from jax.experimental import pallas as pl
from jax.experimental.pallas import tpu as pltpu
from jax.sharding import PartitionSpec as P

HEADS = 20
HEAD_DIM = 112
LANES = 128
LAG = 3
GROUP = 5
TILE = 8
BLOCK = LANES - HEAD_DIM
BODY = HEAD_DIM - BLOCK
MESH = pl.DeviceIdType.MESH
NT = (((1,), (1,)), ((), ()))
TN = (((0,), (0,)), ((), ()))


def dot(a, b, dims=(((1,), (0,)), ((), ()))):
    return lax.dot_general(a, b, dims, preferred_element_type=jnp.float32)


def split(state):
    high = state.astype(jnp.bfloat16)
    return high, (state - high.astype(jnp.float32)).astype(jnp.bfloat16)


def guard(condition, act):
    if condition is True:
        act()
    else:
        pl.when(condition)(act)


def both(*conditions):
    left = [condition for condition in conditions if condition is not True]
    return functools.reduce(jnp.logical_and, left) if left else True


def lanes(rows):
    return lax.broadcasted_iota(jnp.int32, (rows, LANES), 1)


def pack(state, column):
    bottom, spare = state[BODY:], lanes(BLOCK) >= HEAD_DIM
    pieces = [
        jnp.where(spare, pltpu.roll(bottom, HEAD_DIM - at, 1), state[at:at + BLOCK])
        for at in range(0, BODY, BLOCK)
    ]
    lane = lanes(TILE)
    tail = jnp.where(lane >= HEAD_DIM, pltpu.roll(bottom[:TILE], LANES - HEAD_DIM, 1), bottom[TILE:])
    for g in range(HEAD_DIM // TILE):
        tail = jnp.where(lane == g, column[g * TILE:(g + 1) * TILE], tail)
    return jnp.concatenate(pieces + [tail], axis=0)


def unpack(packed, copies):
    tail, lane = packed[BODY:], lanes(BLOCK)
    bottom = jnp.concatenate([pltpu.roll(tail, HEAD_DIM, 1), tail], axis=0)
    pieces = []
    for at in range(0, BODY, BLOCK):
        piece = packed[at:at + BLOCK]
        here = jnp.logical_and(lane >= at, lane < at + BLOCK)
        bottom = jnp.where(here, pltpu.roll(piece, LANES - HEAD_DIM + at, 1), bottom)
        pieces.append(piece)
    pieces.append(bottom)
    whole = []
    for i, piece in enumerate(pieces):
        g = i * BLOCK // TILE
        column = jnp.concatenate([tail[:, g:g + 1], tail[:, g + 1:g + 2]], axis=0)
        z = jnp.where(lane < HEAD_DIM + copies, column, 0.0)
        whole.append(jnp.where(lane < HEAD_DIM, piece, z))
    return jnp.concatenate(whole, axis=0)


def ones_below(tokens):
    row = lax.broadcasted_iota(jnp.int32, (LANES - HEAD_DIM, tokens), 0)
    return row, jnp.where(row < 2, 1.0, 0.0).astype(jnp.bfloat16)


def kernel(
    n_frame, n_space,
    q_in, k_in, v_in, g_in,
    state_out, grad_out, scaled_out,
    qs, ks, vs, gs, scaleds, plain,
    local, prefix, total, arrived, send_sem, recv_sem, in_sem, out_sem,
):
    frame, space = lax.axis_index("frame"), lax.axis_index("space")
    levels = max(n_frame - 1, 0).bit_length()
    right_link, left_link = levels, levels + 1

    def place(phase):
        return frame if phase == 0 else n_frame - 1 - frame

    def partner(phase, level):
        at = place(phase)
        other = at ^ (1 << level)
        upper = lax.rem(at // (1 << level), 2) == 1
        exists = True if n_frame & (n_frame - 1) == 0 else other < n_frame
        sends, receives = exists, exists
        if level == levels - 1:
            sends, receives = both(exists, jnp.logical_not(upper)), both(exists, upper)
        return other if phase == 0 else n_frame - 1 - other, upper, exists, sends, receives

    def link(phase, number, h, source):
        if number == right_link:
            device = (frame, space + 1)
        elif number == left_link:
            device = (frame, space - 1)
        else:
            device = (partner(phase, number)[0], space)
        return pltpu.make_async_remote_copy(
            src_ref=source,
            dst_ref=arrived.at[phase, number, h],
            send_sem=send_sem.at[phase, number, h],
            recv_sem=recv_sem.at[phase, number, h],
            device_id=device,
            device_id_type=MESH,
        )

    barrier = pltpu.get_barrier_semaphore()
    greet = [(space + 1 < n_space, (frame, space + 1)), (space > 0, (frame, space - 1))]
    for phase in (0,) if n_frame & (n_frame - 1) == 0 else (0, 1):
        for level in range(levels):
            other, _, exists, _, _ = partner(phase, level)
            greet.append((exists, (other, space)))
    for exists, device in greet:
        guard(exists, functools.partial(
            pl.semaphore_signal, barrier, inc=1, device_id=device, device_id_type=MESH))

    def load(i, part):
        source, target = ((k_in, ks), (v_in, vs), (q_in, qs), (g_in, gs))[i]
        some = pl.ds(part * GROUP, GROUP)
        return pltpu.make_async_copy(source.at[some], target.at[some], in_sem.at[i, part])

    for pair in ((0, 1), (2, 3)):
        for part in range(HEADS // GROUP):
            for i in pair:
                load(i, part).start()

    def loaded(pair, h):
        @pl.when(lax.rem(h, GROUP) == 0)
        def _():
            for i in pair:
                load(i, h // GROUP).wait()

    def begin(phase, h, value):
        local[phase, h] = value
        if phase == 0:
            begin_chain(phase, h)
        else:
            begin_scan(phase, h)

    def begin_scan(phase, h):
        own = scan_source(phase, 0, h)
        prefix[phase, h] = own[...]
        if levels:
            guard(partner(phase, 0)[3], lambda: link(phase, 0, h, own).start())
        elif phase == 1:
            begin_chain(phase, h)

    def scan_source(phase, level, h):
        if level == 0:
            return (total if phase == 0 else local).at[phase, h]
        return arrived.at[phase, level - 1, h]

    def scan_level(phase, level, h):
        _, upper, exists, sends, receives = partner(phase, level)
        source = scan_source(phase, level, h)

        def take():
            link(phase, level, h, source).wait_recv()
            came = arrived[phase, level, h]
            if level + 1 < levels:
                prefix[phase, h] = prefix[phase, h] + jnp.where(upper, came, 0.0)
                arrived[phase, level, h] = came + source[...]
            else:
                prefix[phase, h] = prefix[phase, h] + came

        guard(receives, take)
        if level + 1 < levels:
            follow = arrived.at[phase, level, h]
            guard(partner(phase, level + 1)[3], lambda: link(phase, level + 1, h, follow).start())
        elif phase == 1:
            begin_chain(phase, h)

    def chain_own(phase, h):
        return (local if phase == 0 else prefix).at[phase, h]

    def begin_chain(phase, h):
        own = chain_own(phase, h)
        total[phase, h] = own[...]
        if n_space > 1:
            guard(space == 0, lambda: link(phase, right_link, h, own).start())
            guard(space == n_space - 1, lambda: link(phase, left_link, h, own).start())

    def chain_hop(phase, number, at, h):
        slot = arrived.at[phase, number, h]
        link(phase, number, h, slot).wait_recv()
        came = slot[...]
        total[phase, h] = total[phase, h] + came

        def forward():
            slot[...] = came + chain_own(phase, h)[...]
            link(phase, number, h, slot).start()

        guard(at < n_space - 1, forward)

    tokens = k_in.shape[2]
    row, ones = ones_below(tokens)

    def values(h):
        return jnp.concatenate([vs[h], ones], axis=0)

    def states(h):
        loaded((0, 1), h)
        state = dot(jnp.maximum(ks[h], 0), values(h), NT)
        begin(0, h, pack(state, state[:, HEAD_DIM:HEAD_DIM + 1]))

    def queries(h):
        loaded((2, 3), h)
        q = jnp.maximum(qs[h], 0)
        state = unpack(prefix[0, h], 2)
        plain[0, h] = state
        store(0, h).start()
        pair = jnp.concatenate(split(state), axis=0)
        numerator = dot(pair, jnp.concatenate([q, q], axis=0), TN)
        inverse = 1.0 / (numerator[HEAD_DIM:HEAD_DIM + 1] + 1.0)
        grad = gs[h].astype(jnp.float32)
        slope = -jnp.sum(grad * numerator[:HEAD_DIM], axis=0, keepdims=True) * inverse * inverse
        coarse = slope.astype(jnp.bfloat16).astype(jnp.float32)
        slopes = jnp.where(row == 0, coarse, jnp.where(row == 1, slope - coarse, 0.0))
        scaled = jnp.concatenate([grad * inverse, slopes], axis=0).astype(jnp.bfloat16)
        grads = dot(q, scaled, NT)
        begin(1, h, pack(grads, grads[:, HEAD_DIM:HEAD_DIM + 1] + grads[:, HEAD_DIM + 1:HEAD_DIM + 2]))
        scaleds[h] = scaled
        store(2, h).start()

    def keys(h):
        plain[1, h] = unpack(total[1, h], 1)
        store(1, h).start()

    def store(i, h):
        source, target = ((plain.at[0], state_out), (plain.at[1], grad_out), (scaleds, scaled_out))[i]
        return pltpu.make_async_copy(source.at[h], target.at[h], out_sem.at[i, h])

    plan = []

    def plan_scan(phase, at):
        for level in range(levels):
            at += LAG - 1 if level == 0 else LAG
            plan.insert(0, (at, True, functools.partial(scan_level, phase, level)))
        return at

    def plan_chain(phase, at):
        for number, place in ((right_link, space), (left_link, n_space - 1 - space)):
            if n_space > 1:
                plan.insert(0, (at + LAG * place, place > 0, functools.partial(chain_hop, phase, number, place)))
        return at + LAG * (n_space - 1)

    turn = plan_chain(0, 0)
    middle = plan_scan(0, turn)
    last = plan_chain(1, plan_scan(1, middle))

    def stage(t, lag, condition, act):
        h = t - lag
        guard(both(h >= 0, h < HEADS, condition), lambda: act(h))

    def step(t, carry):
        for lag, condition, act in plan:
            stage(t, lag, condition, act)
        stage(t, turn, True, functools.partial(begin_scan, 0))
        stage(t, 0, True, states)
        stage(t, middle, True, queries)
        stage(t, last, True, keys)
        return carry

    pl.semaphore_wait(barrier, sum(jnp.int32(exists) for exists, _ in greet))
    lax.fori_loop(0, HEADS + last, step, 0)

    def drain(h, carry):
        for phase in (0, 1):
            for level in range(levels):
                guard(partner(phase, level)[3], link(phase, level, h, scan_source(phase, level, h)).wait_send)
            own = chain_own(phase, h)
            if n_space > 1:
                guard(space < n_space - 1, link(phase, right_link, h, own).wait_send)
                guard(space > 0, link(phase, left_link, h, own).wait_send)
        for i in range(3):
            store(i, h).wait()
        return carry

    lax.fori_loop(0, HEADS, drain, 0)


def products(state, grad, scaled, q, k, v, query_grad, key_grad, value_grad):
    _, ones = ones_below(k.shape[2])
    for h in range(q.shape[0]):
        wide = jnp.concatenate(split(state[h]), axis=1)
        back = dot(wide, jnp.concatenate([scaled[h], scaled[h]], axis=0))
        query_grad[h] = jnp.where(q[h].astype(jnp.float32) > 0, back, 0.0)
        high, low = split(grad[h])
        feature = jnp.maximum(k[h], 0)
        value_grad[h] = dot(
            jnp.concatenate([high[:, :HEAD_DIM], low[:, :HEAD_DIM]], axis=0),
            jnp.concatenate([feature, feature], axis=0), TN)
        value = jnp.concatenate([v[h], ones], axis=0)
        back = dot(jnp.concatenate([high, low], axis=1), jnp.concatenate([value, value], axis=0))
        key_grad[h] = jnp.where(k[h].astype(jnp.float32) > 0, back, 0.0)


def on_device(n_frame, n_space, *arrays):
    rows = arrays[0].shape[1]
    levels = max(n_frame - 1, 0).bit_length()
    heads = [jnp.swapaxes(array[0], 0, 1).reshape(HEADS, HEAD_DIM, rows) for array in arrays]
    shape = heads[0].shape
    state = (HEADS, HEAD_DIM, LANES)
    packed = (HEADS, BODY + TILE, LANES)
    wide = (HEADS, LANES, rows)
    links = (2, levels + 2, HEADS)
    states = pl.pallas_call(
        functools.partial(kernel, n_frame, n_space),
        out_shape=(
            jax.ShapeDtypeStruct(state, jnp.float32),
            jax.ShapeDtypeStruct(state, jnp.float32),
            jax.ShapeDtypeStruct(wide, jnp.bfloat16),
        ),
        in_specs=[pl.BlockSpec(memory_space=pltpu.HBM)] * 4,
        out_specs=(pl.BlockSpec(memory_space=pl.ANY),) * 3,
        scratch_shapes=[pltpu.VMEM(shape, jnp.bfloat16)] * 4 + [pltpu.VMEM(wide, jnp.bfloat16)]
        + [pltpu.VMEM((2,) + state, jnp.float32)] + [pltpu.VMEM((2,) + packed, jnp.float32)] * 3
        + [
            pltpu.VMEM((2, levels + 2) + packed, jnp.float32),
            pltpu.SemaphoreType.DMA(links),
            pltpu.SemaphoreType.DMA(links),
            pltpu.SemaphoreType.DMA((4, HEADS // GROUP)),
            pltpu.SemaphoreType.DMA((3, HEADS)),
        ],
        compiler_params=pltpu.CompilerParams(
            collective_id=0, has_side_effects=True, vmem_limit_bytes=56 * 1024 * 1024
        ),
    )(*heads)
    def some(whole):
        return pl.BlockSpec((GROUP,) + whole[1:], lambda i: (i, 0, 0))

    grads = pl.pallas_call(
        products,
        grid=(HEADS // GROUP,),
        out_shape=(jax.ShapeDtypeStruct(shape, jnp.float32),) * 3,
        in_specs=[some(state), some(state), some(wide)] + [some(shape)] * 3,
        out_specs=(some(shape),) * 3,
        compiler_params=pltpu.CompilerParams(vmem_limit_bytes=56 * 1024 * 1024),
    )(*states, *heads[:3])
    return tuple(jnp.swapaxes(grad.reshape(HEADS * HEAD_DIM, rows), 0, 1)[None] for grad in grads)


def solution(mesh):
    placed = P("frame", "space", None)
    return jax.shard_map(
        functools.partial(on_device, mesh.shape["frame"], mesh.shape["space"]),
        mesh=mesh,
        in_specs=(placed,) * 4,
        out_specs=(placed,) * 3,
        check_vma=False,
    )
```
